32 devices in a mesh: shard: 4 (over y, x), context: 4 (over z), tensor: 2 (over core).
Axes of the slice: x: 2, y: 2, z: 4, core: 2. Of those that a mesh axis runs over, the one named last changes fastest.
Arguments:
- tokens: bfloat16 [4096, 960], P(('shard', 'context', 'tensor')), may hold values from -6 to 6
- cotangent: bfloat16 [4096, 960], P(('shard', 'context', 'tensor')), may hold values from -6 to 6
- lengths: int32 [4, 2], P('shard'), may hold values from 341 to 683, as said below
- qkv_weight: float32 [960, 1600], P('shard'), may hold values from -0.1875 to 0.1875
- qkv_first: float32 [960, 1600], P('shard'), may hold values from -36.48 to 36.48
- qkv_second: float32 [960, 1600], P('shard'), may hold values from 212.992 to 2498.56
- out_weight: float32 [960, 960], P('shard'), may hold values from -3 to 3
- out_first: float32 [960, 960], P('shard'), may hold values from -1.56 to 1.56
- out_second: float32 [960, 960], P('shard'), may hold values from 1.12 to 4.56
- gate_up_weight: float32 [960, 2, 2560], P('shard', None, 'tensor'), may hold values from -0.1875 to 0.1875
- gate_up_first: float32 [960, 2, 2560], P('shard', None, 'tensor'), may hold values from -7.936 to 7.936
- gate_up_second: float32 [960, 2, 2560], P('shard', None, 'tensor'), may hold values from 29.4912 to 118.784
- down_weight: float32 [2560, 960], P('tensor', 'shard'), may hold values from -0.125 to 0.125
- down_first: float32 [2560, 960], P('tensor', 'shard'), may hold values from -12.864 to 12.864
- down_second: float32 [2560, 960], P('tensor', 'shard'), may hold values from 77.4144 to 310.4768
- norm_gains: float32 [2, 960], P(None, 'shard'), may hold values from 0.5 to 1.5
- gains_first: float32 [2, 960], P(None, 'shard'), may hold values from -36.48 to 36.48
- gains_second: float32 [2, 960], P(None, 'shard'), may hold values from 155.648 to 2498.56
Outputs:
- block_out: bfloat16 [4096, 960], P(('shard', 'context', 'tensor'))
- tokens_grad: float32 [4096, 960], P(('shard', 'context', 'tensor'))
- qkv_new: float32 [960, 1600], P('shard')
- qkv_first_new: float32 [960, 1600], P('shard')
- qkv_second_new: float32 [960, 1600], P('shard')
- out_new: float32 [960, 960], P('shard')
- out_first_new: float32 [960, 960], P('shard')
- out_second_new: float32 [960, 960], P('shard')
- gate_up_new: float32 [960, 2, 2560], P('shard', None, 'tensor')
- gate_up_first_new: float32 [960, 2, 2560], P('shard', None, 'tensor')
- gate_up_second_new: float32 [960, 2, 2560], P('shard', None, 'tensor')
- down_new: float32 [2560, 960], P('tensor', 'shard')
- down_first_new: float32 [2560, 960], P('tensor', 'shard')
- down_second_new: float32 [2560, 960], P('tensor', 'shard')
- gains_new: float32 [2, 960], P(None, 'shard')
- gains_first_new: float32 [2, 960], P(None, 'shard')
- gains_second_new: float32 [2, 960], P(None, 'shard')
The draws below stay inside these ranges and needn't reach their ends.
Inputs may be any that keep to these rules, and one draw needn't show every extreme that they name: Each row lists the lengths of the 2 documents of one pack in order; they sum to 1024, each is 341 or more, and the largest over all packs is 683.
All inputs are finite; a program needn't handle non-finite values.
Results may differ from the reference program's by a relative error of at most 0.028.
Values may be sent and summed in bfloat16 or wider, within the bound.
A program may use at most 128 MiB of HBM per device.

```python
import math
import jax
import jax.numpy as jnp
from jax import lax

MODEL_WIDTH = 960
QUERY_HEADS = 15
KEY_VALUE_HEADS = 5
HEAD_SIZE = 64
FF = 2560
STEP = 10
KEY_COLUMNS = 320
QKV = 1600
PACK_TOKENS = 1024
TOKENS = 4096
SHORTEST = 341
N_SHARD = 4


def unit_scale():
    return math.sqrt(TOKENS)


def first_moment(key, array_shape, factor):
    return jax.random.truncated_normal(key, -3.0, 3.0, array_shape, jnp.float32) * (factor / 9.0)


def second_moment(key, array_shape, factor):
    spread = jnp.exp(jax.random.uniform(key, array_shape, jnp.float32, -0.6931, 0.6931))
    return spread * (2.0 * factor * factor / 19.0)


def qkv_columns():
    return jnp.concatenate([jnp.ones((MODEL_WIDTH,), jnp.float32), jnp.full((2 * KEY_COLUMNS,), 1.7, jnp.float32)])[None, :]


def gains_rows():
    return jnp.array([[1.7], [0.85]], jnp.float32)


def draw_lengths(key, part):
    key = jax.random.fold_in(key, 21)
    key_first, key_pack, key_flip = jax.random.split(key, 3)
    leading = jax.random.randint(key_first, (N_SHARD,), SHORTEST, PACK_TOKENS - SHORTEST + 1)
    chosen = jax.random.randint(key_pack, (), 0, N_SHARD)
    flipped = jax.random.randint(key_flip, (), 0, 2)
    forced = SHORTEST + flipped * (PACK_TOKENS - 2 * SHORTEST)
    leading = jnp.where(jnp.arange(N_SHARD) == chosen, forced, leading)
    return jnp.stack([leading, PACK_TOKENS - leading], axis=1).astype(jnp.int32)


def draw_qkv_first(key, part):
    key = jax.random.fold_in(key, 11)
    return first_moment(key, (MODEL_WIDTH, QKV), qkv_columns() * unit_scale())


def draw_qkv_second(key, part):
    key = jax.random.fold_in(key, 12)
    return second_moment(key, (MODEL_WIDTH, QKV), qkv_columns() * unit_scale())


def draw_out_first(key, part):
    key = jax.random.fold_in(key, 13)
    return first_moment(key, (MODEL_WIDTH, MODEL_WIDTH), math.sqrt(5.4 / PACK_TOKENS) * unit_scale())


def draw_out_second(key, part):
    key = jax.random.fold_in(key, 14)
    return second_moment(key, (MODEL_WIDTH, MODEL_WIDTH), math.sqrt(5.4 / PACK_TOKENS) * unit_scale())


def draw_gate_up_first(key, part):
    key = jax.random.fold_in(key, 15)
    return first_moment(key, (MODEL_WIDTH, 2, FF), 0.37 * unit_scale())


def draw_gate_up_second(key, part):
    key = jax.random.fold_in(key, 16)
    return second_moment(key, (MODEL_WIDTH, 2, FF), 0.37 * unit_scale())


def draw_down_first(key, part):
    key = jax.random.fold_in(key, 17)
    return first_moment(key, (FF, MODEL_WIDTH), 0.6 * unit_scale())


def draw_down_second(key, part):
    key = jax.random.fold_in(key, 18)
    return second_moment(key, (FF, MODEL_WIDTH), 0.6 * unit_scale())


def draw_gains_first(key, part):
    key = jax.random.fold_in(key, 19)
    return first_moment(key, (2, MODEL_WIDTH), gains_rows() * unit_scale())


def draw_gains_second(key, part):
    key = jax.random.fold_in(key, 20)
    return second_moment(key, (2, MODEL_WIDTH), gains_rows() * unit_scale())


def steps_of(rng, dims, cuts, least, largest):
    gain = 1.0
    for axis_at, blocks in cuts:
        heights = jax.random.uniform(jax.random.fold_in(jax.random.fold_in(rng, 6), axis_at), (blocks,), jnp.float32, least / len(cuts), largest / len(cuts))
        gain = gain * jnp.repeat(jnp.exp(heights), dims[axis_at] // blocks).reshape((-1,) + (1,) * (len(dims) - 1 - axis_at))
    return gain


def noise(stream_key, dims, scale, reach, pieces=(), kind=jnp.bfloat16):
    values = jax.random.normal(stream_key, dims, jnp.float32) * scale
    if len(pieces) > 0:
        values = steps_of(stream_key, dims, pieces, -0.22, 0.18) * values
    return jnp.clip(values, min=-reach, max=reach).astype(kind)


def setup_inputs(seed: int = 0) -> dict:
    key_of = jax.random.split(jax.random.key(seed), 19)
    tokens = noise(key_of[0], (TOKENS, MODEL_WIDTH), 1.0, 6.0, ((0, 32),))
    cotangent = noise(key_of[1], (TOKENS, MODEL_WIDTH), 1.0, 6.0, ((0, 32),))
    lengths = draw_lengths(jax.random.fold_in(key_of[18], 71), 0)
    qkv_weight = noise(key_of[3], (MODEL_WIDTH, QKV), MODEL_WIDTH ** -0.5, 0.1875, ((0, 4),), jnp.float32)
    qkv_first = draw_qkv_first(jax.random.fold_in(key_of[18], 71), 0)
    qkv_second = draw_qkv_second(jax.random.fold_in(key_of[18], 71), 0)
    out_weight = noise(key_of[6], (MODEL_WIDTH, MODEL_WIDTH), (max(1, 5 * MODEL_WIDTH // PACK_TOKENS)) ** -0.5, 3.0, ((0, 4),), jnp.float32)
    out_first = draw_out_first(jax.random.fold_in(key_of[18], 71), 0)
    out_second = draw_out_second(jax.random.fold_in(key_of[18], 71), 0)
    gate_up_weight = noise(key_of[9], (MODEL_WIDTH, 2, FF), MODEL_WIDTH ** -0.5, 0.1875, ((0, 4), (2, 2)), jnp.float32)
    gate_up_first = draw_gate_up_first(jax.random.fold_in(key_of[18], 71), 0)
    gate_up_second = draw_gate_up_second(jax.random.fold_in(key_of[18], 71), 0)
    down_weight = noise(key_of[12], (FF, MODEL_WIDTH), FF ** -0.5, 0.125, ((0, 2), (1, 4)), jnp.float32)
    down_first = draw_down_first(jax.random.fold_in(key_of[18], 71), 0)
    down_second = draw_down_second(jax.random.fold_in(key_of[18], 71), 0)
    norm_gains = jnp.clip(1.0 + 0.1 * jax.random.normal(key_of[15], (2, MODEL_WIDTH), jnp.float32), 0.5, 1.5)
    gains_first = draw_gains_first(jax.random.fold_in(key_of[18], 71), 0)
    gains_second = draw_gains_second(jax.random.fold_in(key_of[18], 71), 0)
    return dict(tokens=tokens, cotangent=cotangent, lengths=lengths, qkv_weight=qkv_weight, qkv_first=qkv_first, qkv_second=qkv_second, out_weight=out_weight, out_first=out_first, out_second=out_second, gate_up_weight=gate_up_weight, gate_up_first=gate_up_first, gate_up_second=gate_up_second, down_weight=down_weight, down_first=down_first, down_second=down_second, norm_gains=norm_gains, gains_first=gains_first, gains_second=gains_second)


@jax.custom_vjp
def narrow_precision(v):
    return lax.optimization_barrier(v.astype(jnp.bfloat16)).astype(jnp.float32)

@jax.custom_vjp
def low_back(v):
    return v

def low_keep(v):
    return (narrow_precision(v), None)

def low_pass(kept, grad):
    return (grad,)

def back_keep(v):
    return (v, None)

def back_low(kept, grad):
    return (narrow_precision(grad),)
narrow_precision.defvjp(low_keep, low_pass)
low_back.defvjp(back_keep, back_low)
NEGATIVE_HUGE = -1e+30
NORM_EPS = 1e-05
ROPE_BASE = 100000.0
BETA_ONE = 0.9
BETA_TWO = 0.95
ADAM_EPS = 1e-08
RATES = (0.06, 1.0, 0.06, 0.04, 0.4)
DECAYS = (0.1, 0.1, 0.1, 0.1, 0.0)
HIGHEST_PRECISION = lax.Precision.HIGHEST

def rope_angles(position):
    halfway = HEAD_SIZE // 2
    frequency = jnp.exp(jnp.arange(halfway, dtype=jnp.float32) * (-2.0 * math.log(ROPE_BASE) / HEAD_SIZE))
    angles = position.astype(jnp.float32)[:, None] * frequency[None, :]
    return (jnp.cos(angles)[:, None, :], jnp.sin(angles)[:, None, :])

def apply_rotary(vectors, cosine_table, sine_table):
    halfway = HEAD_SIZE // 2
    leading = vectors[..., :halfway]
    trailing = vectors[..., halfway:]
    return jnp.concatenate([leading * cosine_table - trailing * sine_table, trailing * cosine_table + leading * sine_table], axis=-1)

def doc_starts(length_row, row_index):
    doc_ends = jnp.cumsum(length_row)
    before = jnp.where(doc_ends[None, :] <= row_index[:, None], length_row[None, :], 0)
    return lax.optimization_barrier(jnp.sum(before, axis=1)).astype(jnp.int32)

def rms_norm(values, gain_row):
    inverse = lax.rsqrt(lax.optimization_barrier(jnp.mean(values * values, axis=-1, keepdims=True)) + NORM_EPS)
    return values * inverse * gain_row

def adam_step(weight, moment_one, moment_two, gradient, learning, decay_rate):
    first_new = BETA_ONE * moment_one + (1.0 - BETA_ONE) * gradient
    second_new = BETA_TWO * moment_two + (1.0 - BETA_TWO) * gradient * gradient
    first_hat = first_new / (1.0 - BETA_ONE ** STEP)
    second_hat = second_new / (1.0 - BETA_TWO ** STEP)
    weight_new = weight - learning * (first_hat / (jnp.sqrt(second_hat) + ADAM_EPS) + decay_rate * weight)
    return (weight_new, first_new, second_new)

def packed_attention(pack_item):
    query_rows, rows_of_keys, rows_of_values, start_positions = pack_item
    count_of_rows = query_rows.shape[0]
    rows_per_block = min(512, count_of_rows)
    column_index = jnp.arange(count_of_rows, dtype=jnp.int32)

    def one_block(block_item):
        query_block, start_block, index_block = block_item
        scores = jnp.einsum('qhgd,khd->qhgk', query_block, rows_of_keys, precision=HIGHEST_PRECISION) * (1.0 / math.sqrt(HEAD_SIZE))
        scores = low_back(scores)
        visible = (column_index[None, :] >= start_block[:, None]) & (column_index[None, :] <= index_block[:, None])
        masked = jnp.where(visible[:, None, None, :], scores, NEGATIVE_HUGE)
        softmax_rows = jnp.exp(masked - jax.nn.logsumexp(masked, axis=-1, keepdims=True))
        return jnp.einsum('qhgk,khd->qhgd', narrow_precision(softmax_rows), rows_of_values, precision=HIGHEST_PRECISION)
    count_of_blocks = count_of_rows // rows_per_block
    pack_groups = QUERY_HEADS // KEY_VALUE_HEADS
    pack_entries = (query_rows.reshape(count_of_blocks, rows_per_block, KEY_VALUE_HEADS, pack_groups, HEAD_SIZE), start_positions.reshape(count_of_blocks, rows_per_block), column_index.reshape(count_of_blocks, rows_per_block))
    return lax.map(jax.checkpoint(one_block), pack_entries).reshape(count_of_rows, MODEL_WIDTH)

def layer(inputs, qkv_weight, out_weight, gate_up_weight, down_weight, norm_gains, lengths):
    gains_low = narrow_precision(norm_gains)
    count_of_rows = inputs.shape[0]
    pack_groups = QUERY_HEADS // KEY_VALUE_HEADS
    normed_one = narrow_precision(rms_norm(inputs, gains_low[0]))
    projected_output = jnp.dot(normed_one, narrow_precision(qkv_weight), precision=HIGHEST_PRECISION)
    query_rows = low_back(projected_output[:, :MODEL_WIDTH])
    rows_of_keys = low_back(projected_output[:, MODEL_WIDTH:MODEL_WIDTH + KEY_COLUMNS])
    rows_of_values = narrow_precision(low_back(projected_output[:, MODEL_WIDTH + KEY_COLUMNS:]))
    pack_index = jnp.arange(PACK_TOKENS, dtype=jnp.int32)
    start_positions = jax.vmap(doc_starts, in_axes=(0, None))(lengths, pack_index)
    position = jnp.tile(pack_index, N_SHARD) - start_positions.reshape(count_of_rows)
    cosine_table, sine_table = rope_angles(position)
    query_rows = narrow_precision(apply_rotary(query_rows.reshape(count_of_rows, QUERY_HEADS, HEAD_SIZE), cosine_table, sine_table))
    rows_of_keys = narrow_precision(apply_rotary(rows_of_keys.reshape(count_of_rows, KEY_VALUE_HEADS, HEAD_SIZE), cosine_table, sine_table))
    attended_rows = lax.map(packed_attention, (query_rows.reshape(N_SHARD, PACK_TOKENS, KEY_VALUE_HEADS, pack_groups, HEAD_SIZE), rows_of_keys.reshape(N_SHARD, PACK_TOKENS, KEY_VALUE_HEADS, HEAD_SIZE), rows_of_values.reshape(N_SHARD, PACK_TOKENS, KEY_VALUE_HEADS, HEAD_SIZE), start_positions))
    attended_rows = narrow_precision(low_back(attended_rows.reshape(count_of_rows, MODEL_WIDTH)))
    residual = inputs + low_back(jnp.dot(attended_rows, narrow_precision(out_weight), precision=HIGHEST_PRECISION))
    normed_two = narrow_precision(rms_norm(residual, gains_low[1]))
    gate_up = low_back(jnp.einsum('td,dcf->tcf', normed_two, narrow_precision(gate_up_weight), precision=HIGHEST_PRECISION))
    hidden = narrow_precision(jax.nn.silu(gate_up[:, 0]) * gate_up[:, 1])
    return residual + jnp.dot(hidden, narrow_precision(down_weight), precision=HIGHEST_PRECISION)

def reference(tokens, cotangent, lengths, qkv_weight, qkv_first, qkv_second, out_weight, out_first, out_second, gate_up_weight, gate_up_first, gate_up_second, down_weight, down_first, down_second, norm_gains, gains_first, gains_second):
    inputs = tokens.astype(jnp.float32)

    def forward(inputs_f, qkv_w, out_w, gate_up_w, down_w, gains_w):
        return layer(inputs_f, qkv_w, out_w, gate_up_w, down_w, gains_w, lengths)
    block_out, pullback = jax.vjp(forward, inputs, qkv_weight, out_weight, gate_up_weight, down_weight, norm_gains)
    gradients = pullback(cotangent.astype(jnp.float32))
    qkv_set = adam_step(qkv_weight, qkv_first, qkv_second, gradients[1], RATES[0], DECAYS[0])
    out_set = adam_step(out_weight, out_first, out_second, gradients[2], RATES[1], DECAYS[1])
    gate_up_set = adam_step(gate_up_weight, gate_up_first, gate_up_second, gradients[3], RATES[2], DECAYS[2])
    down_set = adam_step(down_weight, down_first, down_second, gradients[4], RATES[3], DECAYS[3])
    gains_set = adam_step(norm_gains, gains_first, gains_second, gradients[5], RATES[4], DECAYS[4])
    return (block_out.astype(jnp.bfloat16), gradients[0], qkv_set[0], qkv_set[1], qkv_set[2], out_set[0], out_set[1], out_set[2], gate_up_set[0], gate_up_set[1], gate_up_set[2], down_set[0], down_set[1], down_set[2], gains_set[0], gains_set[1], gains_set[2])
```

```python
import functools
import math

import jax
import jax.numpy as jnp
from jax import lax
from jax.experimental import pallas as pl
from jax.experimental.pallas import tpu as pltpu
from jax.sharding import PartitionSpec as P

MODEL_WIDTH = 960
QUERY_HEADS = 15
KEY_VALUE_HEADS = 5
HEAD_SIZE = 64
STEP = 10
KEY_COLUMNS = 320


NEGATIVE_HUGE = -1e30
NORM_EPS = 1e-05
ROPE_BASE = 100000.0
BETA_ONE = 0.9
BETA_TWO = 0.95
ADAM_EPS = 1e-08
RATES = (0.06, 1.0, 0.06, 0.04, 0.4)
DECAYS = (0.1, 0.1, 0.1, 0.1, 0.0)


MESH = pl.DeviceIdType.MESH
BF16 = jnp.bfloat16
GAIN_ROWS = 16
ROW_CHUNKS = 3


def plane_peers():
    s = lax.axis_index("shard")
    c = lax.axis_index("context")
    t = lax.axis_index("tensor")
    x, y = lax.rem(s, 2), s // 2
    across, along, diagonal = 2 * y + 1 - x, 2 * (1 - y) + x, 2 * (1 - y) + 1 - x
    return s, c, t, across, along, diagonal


def greet(devices):
    barrier = pltpu.get_barrier_semaphore()
    for device in devices:
        pl.semaphore_signal(barrier, inc=1, device_id=device, device_id_type=MESH)
    pl.semaphore_wait(barrier, len(devices))


def gather_kernel(w, gains, out, gains_out, send, recv, local):
    s, c, t, across, along, diagonal = plane_peers()
    to_x, to_y, to_d, to_core = (across, c, t), (along, c, t), (diagonal, c, t), (s, c, 1 - t)
    greet((to_x, to_y, to_d, to_core))

    def block(k):
        return t if k == 0 else k + 1

    def copy(src, dst, lane, k, device):
        return pltpu.make_async_remote_copy(
            src_ref=src,
            dst_ref=dst,
            send_sem=send.at[lane, k],
            recv_sem=recv.at[lane, k],
            device_id=device,
            device_id_type=MESH,
        )

    def own(lane, k):
        return copy(w.at[block(k)], out.at[block(k), s], lane, k, (to_x, to_y)[lane])

    def onward(k):
        if k < 2:
            place = out.at[block(k), across]
            return copy(place, place, 2, k, to_y)
        place = out.at[block(k), along]
        return copy(place, place, 2, k, to_x)

    def sideways(i):
        place = out.at[t, (across, along, diagonal)[i]]
        return copy(place, place, 3, i, to_core)

    def small(i):
        return copy(gains, gains_out.at[s], 4, i, (to_x, to_y, to_d)[i])

    keep = pltpu.make_async_copy(w, out.at[:, s], local.at[0])
    keep_gains = pltpu.make_async_copy(gains, gains_out.at[s], local.at[1])
    for i in range(3):
        small(i).start()
    for k in range(4):
        own(0, k).start()
        own(1, (k + 2) % 4).start()
    keep.start()
    keep_gains.start()
    for k in range(2):
        own(0, k).wait_recv()
        onward(k).start()
        if k == 0:
            sideways(0).start()
        own(1, k + 2).wait_recv()
        onward(k + 2).start()
    own(1, 0).wait_recv()
    sideways(1).start()
    own(1, 1).wait_recv()
    own(0, 2).wait_recv()
    own(0, 3).wait_recv()
    onward(0).wait_recv()
    sideways(2).start()
    for k in range(1, 4):
        onward(k).wait_recv()
    for i in range(3):
        sideways(i).wait_recv()
        small(i).wait_recv()
    for k in range(4):
        own(0, k).wait_send()
        own(1, k).wait_send()
        onward(k).wait_send()
    for i in range(3):
        sideways(i).wait_send()
        small(i).wait_send()
    keep.wait()
    keep_gains.wait()


def gather_weights(w, gains):
    blocks, rows, cols = w.shape
    return pl.pallas_call(
        gather_kernel,
        out_shape=(
            jax.ShapeDtypeStruct((blocks, 4, rows, cols), BF16),
            jax.ShapeDtypeStruct((4,) + gains.shape, BF16),
        ),
        in_specs=[pl.BlockSpec(memory_space=pl.ANY)] * 2,
        out_specs=[pl.BlockSpec(memory_space=pl.ANY)] * 2,
        scratch_shapes=[
            pltpu.SemaphoreType.DMA((5, 4)),
            pltpu.SemaphoreType.DMA((5, 4)),
            pltpu.SemaphoreType.DMA((2,)),
        ],
        compiler_params=pltpu.CompilerParams(collective_id=0, has_side_effects=True),
        name="gather_weights",
    )(w, gains)


def reduce_kernel(
    n, chunks, attn, ffn, attn_out, ffn_out, side, first, partial, direct, summed, line, middle, carry, send, recv
):
    s, c, t, across, along, diagonal = plane_peers()
    half = n // 2
    low = c < half
    inner = jnp.where(low, c + 1, c - 1)
    outer = jnp.where(low, c - 1, c + 1)
    to_x, to_y, to_core = (across, c, t), (along, c, t), (s, c, 1 - t)
    at_end = (c == 0) | (c == n - 1)
    at_middle = (c == half - 1) | (c == half)
    barrier = pltpu.get_barrier_semaphore()
    for device in (to_x, to_y, to_core, (s, inner, t)):
        pl.semaphore_signal(barrier, inc=1, device_id=device, device_id_type=MESH)

    @pl.when(jnp.logical_not(at_end))
    def _():
        pl.semaphore_signal(barrier, inc=1, device_id=(s, outer, t), device_id_type=MESH)
        pl.semaphore_wait(barrier, 5)

    @pl.when(at_end)
    def _():
        pl.semaphore_wait(barrier, 4)

    def copy(src, dst, lane, i, device):
        return pltpu.make_async_remote_copy(
            src_ref=src,
            dst_ref=dst,
            send_sem=send.at[lane, i],
            recv_sem=recv.at[lane, i],
            device_id=device,
            device_id_type=MESH,
        )

    def rows_of(i, buffer):
        return buffer.at[i, pl.ds(0, chunks[i][2])]

    def mine(i, owner):
        k, start, size = chunks[i]
        if k == 0:
            return side.at[owner, pl.ds(start, size)]
        return ffn.at[k - 1, owner, pl.ds(start, size)]

    def result(i):
        k, start, size = chunks[i]
        if k == 0:
            return attn_out.at[t, pl.ds(start, size)]
        return ffn_out.at[k - 1, pl.ds(start, size)]

    def x_first(i):
        return chunks[i][0] < 2

    def add(*refs):
        total = refs[0][...].astype(jnp.float32)
        for ref in refs[1:]:
            total = total + ref[...].astype(jnp.float32)
        return total.astype(BF16)

    def send_first(i):
        return copy(mine(i, diagonal), rows_of(i, first), 0, i, to_x if x_first(i) else to_y)

    def send_direct(i):
        owner, device = (across, to_x) if x_first(i) else (along, to_y)
        return copy(mine(i, owner), rows_of(i, direct), 1, i, device)

    def send_summed(i):
        return copy(rows_of(i, partial), rows_of(i, summed), 2, i, to_y if x_first(i) else to_x)

    def send_in(i):
        return copy(rows_of(i, carry), rows_of(i, line), 3, i, (s, inner, t))

    def send_middle(i):
        return copy(rows_of(i, carry), rows_of(i, middle), 4, i, (s, inner, t))

    def send_out(i):
        return copy(result(i), result(i), 5, i, (s, outer, t))

    def send_core(i):
        return copy(result(i), result(i), 6, i, to_core)

    def send_side():
        return copy(attn.at[1 - t], side, 7, 0, to_core)

    count = len(chunks)
    send_side().start()
    for i in range(count):
        if chunks[i][0] != 0:
            send_first(i).start()
            send_direct(i).start()

    send_side().wait()
    for owner in range(4):
        side[owner] = add(attn.at[t, owner], side.at[owner])
    for i in range(count):
        if chunks[i][0] == 0:
            send_first(i).start()
            send_direct(i).start()

    def stage_plane(i):
        send_first(i).wait_recv()
        owner = along if x_first(i) else across
        partial[i, pl.ds(0, chunks[i][2])] = add(mine(i, owner), rows_of(i, first))
        send_summed(i).start()

    def stage_in(i):
        send_direct(i).wait_recv()
        send_summed(i).wait_recv()
        carry[i, pl.ds(0, chunks[i][2])] = add(mine(i, s), rows_of(i, direct), rows_of(i, summed))

        @pl.when(at_end)
        def _():
            send_in(i).start()

    def stage_fold(i):
        @pl.when(jnp.logical_not(at_end))
        def _():
            send_in(i).wait_recv()
            carry[i, pl.ds(0, chunks[i][2])] = add(rows_of(i, carry), rows_of(i, line))

            @pl.when(at_middle)
            def _():
                send_middle(i).start()

            @pl.when(jnp.logical_not(at_middle))
            def _():
                send_in(i).start()

    def stage_total(i):
        @pl.when(at_middle)
        def _():
            send_middle(i).wait()
            result(i)[...] = add(rows_of(i, carry), rows_of(i, middle))

        @pl.when(jnp.logical_not(at_middle))
        def _():
            send_out(i).wait_recv()
            send_in(i).wait_send()

        @pl.when(jnp.logical_not(at_end))
        def _():
            send_out(i).start()

        if chunks[i][0] == 0:
            send_core(i).start()

    stages = (stage_plane, stage_in, stage_fold, stage_total)
    for step in range(count + len(stages) - 1):
        for depth, stage in enumerate(stages):
            if 0 <= step - depth < count:
                stage(step - depth)
    for i in range(count):
        send_first(i).wait_send()
        send_direct(i).wait_send()
        send_summed(i).wait_send()

        @pl.when(jnp.logical_not(at_end))
        def _():
            send_out(i).wait_send()

        if chunks[i][0] == 0:
            send_core(i).wait()


def reduce_grads(n, attn, ffn):
    attn_rows, ffn_rows, cols = attn.shape[2], ffn.shape[2], attn.shape[3]
    chunks = []
    step = ffn_rows // ROW_CHUNKS
    tail = attn_rows - step * (ROW_CHUNKS - 1)
    for k in (1, 2, 3, 0):
        for j in range(ROW_CHUNKS):
            chunks.append((k, j * step, tail if k == 0 and j == ROW_CHUNKS - 1 else step))
    order = [i for pair in zip(range(ROW_CHUNKS), range(ROW_CHUNKS, 2 * ROW_CHUNKS)) for i in pair]
    order = order + list(range(2 * ROW_CHUNKS, 4 * ROW_CHUNKS))
    chunks = [chunks[i] for i in order]
    count, most = len(chunks), max(step, tail)
    held = pltpu.VMEM((count, most, cols), BF16)
    return pl.pallas_call(
        functools.partial(reduce_kernel, n, tuple(chunks)),
        out_shape=(
            jax.ShapeDtypeStruct((2, attn_rows, cols), BF16),
            jax.ShapeDtypeStruct((3, ffn_rows, cols), BF16),
        ),
        in_specs=[pl.BlockSpec(memory_space=pltpu.VMEM)] * 2,
        out_specs=[pl.BlockSpec(memory_space=pltpu.VMEM)] * 2,
        scratch_shapes=[pltpu.VMEM((4, attn_rows, cols), BF16)]
        + [held] * 7
        + [pltpu.SemaphoreType.DMA((8, count)), pltpu.SemaphoreType.DMA((8, count))],
        compiler_params=pltpu.CompilerParams(
            collective_id=1, has_side_effects=True, vmem_limit_bytes=56 * 1024 * 1024
        ),
        name="reduce_grads",
    )(attn, ffn)


def rope_angles(position):
    halfway = HEAD_SIZE // 2
    frequency = jnp.exp(
        jnp.arange(halfway, dtype=jnp.float32) * (-2.0 * math.log(ROPE_BASE) / HEAD_SIZE)
    )
    angles = position.astype(jnp.float32)[:, None] * frequency[None, :]
    return (jnp.cos(angles)[:, None, :], jnp.sin(angles)[:, None, :])


def apply_rotary(vectors, cosine_table, sine_table):
    halfway = HEAD_SIZE // 2
    leading = vectors[..., :halfway]
    trailing = vectors[..., halfway:]
    return jnp.concatenate(
        [
            leading * cosine_table - trailing * sine_table,
            trailing * cosine_table + leading * sine_table,
        ],
        axis=-1,
    )


def unrotate(gradient, cosine_table, sine_table):
    halfway = HEAD_SIZE // 2
    leading = gradient[..., :halfway]
    trailing = gradient[..., halfway:]
    return jnp.concatenate(
        [
            leading * cosine_table + trailing * sine_table,
            trailing * cosine_table - leading * sine_table,
        ],
        axis=-1,
    )


def doc_starts(length_row, row_index):
    doc_ends = jnp.cumsum(length_row)
    before = jnp.where(doc_ends[None, :] <= row_index[:, None], length_row[None, :], 0)
    return jnp.sum(before, axis=1)


def rms_norm(values, gain_row):
    inverse = lax.rsqrt(jnp.mean(values * values, axis=-1, keepdims=True) + NORM_EPS)
    return (values * inverse * gain_row, inverse)


def norm_back(values, inverse, gain_row, gradient):
    unit_values = values * inverse
    scaled = gradient * gain_row
    gain_grad = jnp.sum(gradient * unit_values, axis=0)
    values_grad = inverse * (
        scaled - unit_values * jnp.mean(scaled * unit_values, axis=-1, keepdims=True)
    )
    return (gain_grad, values_grad)


def adam_step(weight, moment_one, moment_two, gradient, learning, decay_rate):
    first_new = BETA_ONE * moment_one + (1.0 - BETA_ONE) * gradient
    second_new = BETA_TWO * moment_two + (1.0 - BETA_TWO) * gradient * gradient
    first_hat = first_new / (1.0 - BETA_ONE**STEP)
    second_hat = second_new / (1.0 - BETA_TWO**STEP)
    weight_new = weight - learning * (
        first_hat / (jnp.sqrt(second_hat) + ADAM_EPS) + decay_rate * weight
    )
    return (weight_new, first_new, second_new)


def block_scores(query_low, key_block, row_index, row_start, block_id):
    rows_per_block = key_block.shape[0]
    scores = jnp.einsum(
        "qhgd,khd->qhgk", query_low, key_block, preferred_element_type=jnp.float32
    ) * (1.0 / math.sqrt(HEAD_SIZE))
    column_index = block_id * rows_per_block + jnp.arange(rows_per_block, dtype=jnp.int32)
    visible = (column_index[None, :] >= row_start[:, None]) & (
        column_index[None, :] <= row_index[:, None]
    )
    return (scores, visible[:, None, None, :])


def shards(
    tokens,
    cotangent,
    lengths,
    qkv_weight,
    qkv_first,
    qkv_second,
    out_weight,
    out_first,
    out_second,
    gate_up_weight,
    gate_up_first,
    gate_up_second,
    down_weight,
    down_first,
    down_second,
    norm_gains,
    gains_first,
    gains_second,
):
    shard_rows = tokens.shape[0]
    pack_groups = QUERY_HEADS // KEY_VALUE_HEADS
    qkv_low = qkv_weight.astype(jnp.bfloat16)
    out_low = out_weight.astype(jnp.bfloat16)
    gate_up_low = gate_up_weight.astype(jnp.bfloat16)
    down_low = down_weight.astype(jnp.bfloat16)
    gains_low = norm_gains.astype(jnp.bfloat16)
    plane = lax.axis_size("shard") == 4 and lax.axis_size("context") % 2 == 0
    width, hidden_units = MODEL_WIDTH + KEY_COLUMNS, down_weight.shape[0]
    plane = plane and hidden_units == width
    if plane:
        weights = jnp.stack(
            [
                qkv_low[:, :width],
                jnp.concatenate([qkv_low[:, width:], out_low], axis=1),
                gate_up_low[:, 0],
                gate_up_low[:, 1],
                down_low.T,
            ]
        )
        own_gains = jnp.pad(gains_low, ((0, GAIN_ROWS - 2), (0, 0)))
        gathered, gains_parts = gather_weights(weights, own_gains)
        gathered = gathered.reshape(5, MODEL_WIDTH, width)
        qkv_mat = jnp.concatenate([gathered[0], gathered[1, :, :KEY_COLUMNS]], axis=1)
        out_mat = gathered[1, :, KEY_COLUMNS:]
        gate_mat, up_mat, down_mat_t = gathered[2], gathered[3], gathered[4]
        gains_all = gains_parts[:, :2].transpose(1, 0, 2).reshape(2, MODEL_WIDTH)
    else:
        qkv_mat = lax.all_gather(qkv_low, "shard", axis=0, tiled=True)
        out_mat = lax.all_gather(out_low, "shard", axis=0, tiled=True)
        gate_up_mat = lax.all_gather(gate_up_low, "shard", axis=0, tiled=True)
        gate_mat, up_mat = gate_up_mat[:, 0], gate_up_mat[:, 1]
        down_mat_t = lax.all_gather(down_low, "shard", axis=1, tiled=True).T
        gains_all = lax.all_gather(gains_low, "shard", axis=1, tiled=True)
    gains_full = gains_all.astype(jnp.float32)
    tensor_size = lax.axis_size("tensor")
    offset = (lax.axis_index("context") * tensor_size + lax.axis_index("tensor")) * shard_rows
    row_index = offset + jnp.arange(shard_rows, dtype=jnp.int32)
    row_start = doc_starts(lengths[0], row_index)
    cosine_table, sine_table = rope_angles(row_index - row_start)
    inputs = tokens.astype(jnp.float32)
    normed_one, inverse_one = rms_norm(inputs, gains_full[0])
    first_low = normed_one.astype(jnp.bfloat16)
    projected_output = jnp.dot(first_low, qkv_mat, preferred_element_type=jnp.float32)
    query_low = (
        apply_rotary(
            projected_output[:, :MODEL_WIDTH].reshape(shard_rows, QUERY_HEADS, HEAD_SIZE),
            cosine_table,
            sine_table,
        )
        .astype(jnp.bfloat16)
        .reshape(shard_rows, KEY_VALUE_HEADS, pack_groups, HEAD_SIZE)
    )
    keys_low = (
        apply_rotary(
            projected_output[:, MODEL_WIDTH : MODEL_WIDTH + KEY_COLUMNS].reshape(
                shard_rows, KEY_VALUE_HEADS, HEAD_SIZE
            ),
            cosine_table,
            sine_table,
        )
        .astype(jnp.bfloat16)
        .reshape(shard_rows, KEY_COLUMNS)
    )
    kv_local = jnp.concatenate(
        [keys_low, projected_output[:, MODEL_WIDTH + KEY_COLUMNS :].astype(jnp.bfloat16)], axis=1
    )
    key_value_whole = lax.all_gather(kv_local, ("context", "tensor"), axis=0, tiled=True)
    total_keys = key_value_whole.shape[0]
    rows_per_block = min(512, total_keys)
    count_of_blocks = total_keys // rows_per_block
    key_value_blocks = key_value_whole.reshape(
        count_of_blocks, rows_per_block, 2, KEY_VALUE_HEADS, HEAD_SIZE
    )
    block_numbers = jnp.arange(count_of_blocks, dtype=jnp.int32)

    def scan_total(scan_carry, scan_item):
        running, running_sum = scan_carry
        block_id, kv_block = scan_item
        scores, visible = block_scores(query_low, kv_block[:, 0], row_index, row_start, block_id)
        masked = jnp.where(visible, scores, NEGATIVE_HUGE)
        highest = jnp.maximum(running, jnp.max(masked, axis=-1))
        exponent = jnp.where(visible, jnp.exp(masked - highest[..., None]), 0.0)
        running_sum = running_sum * jnp.exp(running - highest) + jnp.sum(exponent, axis=-1)
        return ((highest, running_sum), None)

    latest_start = jnp.full((shard_rows, KEY_VALUE_HEADS, pack_groups), NEGATIVE_HUGE, jnp.float32)
    (running, running_sum), unused = lax.scan(
        scan_total, (latest_start, jnp.zeros_like(latest_start)), (block_numbers, key_value_blocks)
    )
    log_total = running + jnp.log(running_sum)

    def sweep_output(accumulated, scan_item):
        block_id, kv_block = scan_item
        scores, visible = block_scores(query_low, kv_block[:, 0], row_index, row_start, block_id)
        softmax_rows = jnp.where(visible, jnp.exp(scores - log_total[..., None]), 0.0)
        accumulated = accumulated + jnp.einsum(
            "qhgk,khd->qhgd",
            softmax_rows.astype(jnp.bfloat16),
            kv_block[:, 1],
            preferred_element_type=jnp.float32,
        )
        return (accumulated, None)

    attended_heads, unused = lax.scan(
        sweep_output,
        jnp.zeros((shard_rows, KEY_VALUE_HEADS, pack_groups, HEAD_SIZE), jnp.float32),
        (block_numbers, key_value_blocks),
    )
    attended_low = attended_heads.reshape(shard_rows, MODEL_WIDTH).astype(jnp.bfloat16)
    branch = jnp.dot(attended_low, out_mat, preferred_element_type=jnp.float32)
    hidden_state = inputs + branch
    normed_two, inverse_two = rms_norm(hidden_state, gains_full[1])
    second_low = normed_two.astype(jnp.bfloat16)
    ffn_rows = lax.all_gather(second_low, "tensor", axis=0, tiled=True)
    gate_vals = jnp.dot(ffn_rows, gate_mat, preferred_element_type=jnp.float32)
    upward = jnp.dot(ffn_rows, up_mat, preferred_element_type=jnp.float32)
    gate_sigmoid = jax.nn.sigmoid(gate_vals)
    activated = gate_vals * gate_sigmoid
    hidden_low = (activated * upward).astype(jnp.bfloat16)
    partial_out = jnp.einsum("tf,df->td", hidden_low, down_mat_t, preferred_element_type=jnp.float32)
    ffn_out = lax.psum_scatter(
        partial_out.astype(jnp.bfloat16), "tensor", scatter_dimension=0, tiled=True
    ).astype(jnp.float32)
    block_out = (hidden_state + ffn_out).astype(jnp.bfloat16)
    grad_rows = lax.all_gather(cotangent, "tensor", axis=0, tiled=True)
    down_grad_t = jnp.einsum("td,tf->df", grad_rows, hidden_low, preferred_element_type=jnp.float32)
    hidden_grad = jnp.dot(grad_rows, down_mat_t, preferred_element_type=jnp.float32)
    gate_grad = hidden_grad * upward * gate_sigmoid * (1.0 + gate_vals * (1.0 - gate_sigmoid))
    upward_grad = hidden_grad * activated
    gate_grad_low = gate_grad.astype(jnp.bfloat16)
    upward_grad_low = upward_grad.astype(jnp.bfloat16)
    gate_grad = jnp.einsum("td,tf->df", ffn_rows, gate_grad_low, preferred_element_type=jnp.float32)
    upward_grad = jnp.einsum(
        "td,tf->df", ffn_rows, upward_grad_low, preferred_element_type=jnp.float32
    )
    normed_part = jnp.einsum(
        "tf,df->td", gate_grad_low, gate_mat, preferred_element_type=jnp.float32
    ) + jnp.einsum("tf,df->td", upward_grad_low, up_mat, preferred_element_type=jnp.float32)
    normed_two_grad = lax.psum_scatter(
        normed_part.astype(jnp.bfloat16), "tensor", scatter_dimension=0, tiled=True
    ).astype(jnp.float32)
    gain_two_grad, state_norm_grad = norm_back(
        hidden_state, inverse_two, gains_full[1], normed_two_grad
    )
    state_grad = cotangent.astype(jnp.float32) + state_norm_grad
    branch_low = state_grad.astype(jnp.bfloat16)
    out_grad = jnp.einsum("tk,td->kd", attended_low, branch_low, preferred_element_type=jnp.float32)
    attended_gradient = jnp.einsum(
        "td,kd->tk", branch_low, out_mat, preferred_element_type=jnp.float32
    )
    attended_gradient_narrow = attended_gradient.astype(jnp.bfloat16).reshape(
        shard_rows, KEY_VALUE_HEADS, pack_groups, HEAD_SIZE
    )
    delta_rows = jnp.sum(attended_gradient_narrow.astype(jnp.float32) * attended_heads, axis=-1)

    def sweep_backward(query_grad, scan_item):
        block_id, kv_block = scan_item
        scores, visible = block_scores(query_low, kv_block[:, 0], row_index, row_start, block_id)
        softmax_rows = jnp.where(visible, jnp.exp(scores - log_total[..., None]), 0.0)
        softmax_low = softmax_rows.astype(jnp.bfloat16)
        probs_grad = jnp.einsum(
            "qhgd,khd->qhgk",
            attended_gradient_narrow,
            kv_block[:, 1],
            preferred_element_type=jnp.float32,
        )
        scores_low = (softmax_rows * (probs_grad - delta_rows[..., None])).astype(jnp.bfloat16)
        query_grad = query_grad + jnp.einsum(
            "qhgk,khd->qhgd", scores_low, kv_block[:, 0], preferred_element_type=jnp.float32
        ) * (1.0 / math.sqrt(HEAD_SIZE))
        key_grad = jnp.einsum(
            "qhgk,qhgd->khd", scores_low, query_low, preferred_element_type=jnp.float32
        ) * (1.0 / math.sqrt(HEAD_SIZE))
        value_grad = jnp.einsum(
            "qhgk,qhgd->khd",
            softmax_low,
            attended_gradient_narrow,
            preferred_element_type=jnp.float32,
        )
        return (query_grad, jnp.stack([key_grad, value_grad], axis=1))

    query_grad, kv_terms = lax.scan(
        sweep_backward,
        jnp.zeros((shard_rows, KEY_VALUE_HEADS, pack_groups, HEAD_SIZE), jnp.float32),
        (block_numbers, key_value_blocks),
    )
    kv_terms = kv_terms.reshape(total_keys, 2 * KEY_COLUMNS)
    key_value_gradient = lax.psum_scatter(
        kv_terms.astype(jnp.bfloat16), ("context", "tensor"), scatter_dimension=0, tiled=True
    ).astype(jnp.float32)
    key_back = unrotate(
        key_value_gradient[:, :KEY_COLUMNS].reshape(shard_rows, KEY_VALUE_HEADS, HEAD_SIZE),
        cosine_table,
        sine_table,
    ).reshape(shard_rows, KEY_COLUMNS)
    query_back = unrotate(
        query_grad.reshape(shard_rows, QUERY_HEADS, HEAD_SIZE), cosine_table, sine_table
    ).reshape(shard_rows, MODEL_WIDTH)
    projected_low = jnp.concatenate(
        [query_back, key_back, key_value_gradient[:, KEY_COLUMNS:]], axis=1
    ).astype(jnp.bfloat16)
    qkv_grad = jnp.einsum("td,tk->dk", first_low, projected_low, preferred_element_type=jnp.float32)
    normed_one_grad = jnp.einsum(
        "tk,dk->td", projected_low, qkv_mat, preferred_element_type=jnp.float32
    )
    gain_one_grad, input_norm_grad = norm_back(inputs, inverse_one, gains_full[0], normed_one_grad)
    tokens_grad = state_grad + input_norm_grad
    gains_grad = jnp.stack([gain_one_grad, gain_two_grad])
    if plane:
        rows = MODEL_WIDTH // 4
        attn_grad = jnp.stack(
            [
                qkv_grad[:, :width].astype(jnp.bfloat16),
                jnp.concatenate([qkv_grad[:, width:], out_grad], axis=1).astype(jnp.bfloat16),
            ]
        ).reshape(2, 4, rows, width)
        gain_rows = jnp.pad(
            gains_grad.astype(jnp.bfloat16).reshape(2, 4, rows).transpose(1, 0, 2),
            ((0, 0), (0, GAIN_ROWS - 2), (0, width - rows)),
        )
        gain_rows = jnp.stack([gain_rows, jnp.zeros_like(gain_rows)])
        attn_grad = jnp.concatenate([attn_grad, gain_rows], axis=2)
        ffn_grad = jnp.stack(
            [part.astype(jnp.bfloat16) for part in (gate_grad, upward_grad, down_grad_t)]
        ).reshape(3, 4, rows, width)
        attn_red, ffn_red = reduce_grads(lax.axis_size("context"), attn_grad, ffn_grad)
        gains_red = attn_red[0, rows : rows + 2, :rows].astype(jnp.float32)
        qkv_red = jnp.concatenate(
            [attn_red[0, :rows], attn_red[1, :rows, :KEY_COLUMNS]], axis=1
        ).astype(jnp.float32)
        out_red = attn_red[1, :rows, KEY_COLUMNS:].astype(jnp.float32)
        gate_up_red = jnp.stack([ffn_red[0], ffn_red[1]], axis=1).astype(jnp.float32)
        down_red = ffn_red[2].T.astype(jnp.float32)
    else:
        gate_up_grad = jnp.stack([gate_grad, upward_grad], axis=1)
        down_grad = down_grad_t.T
        qkv_part, out_part, gate_up_part, down_part, gains_part = (
            lax.psum_scatter(
                qkv_grad.astype(jnp.bfloat16), "shard", scatter_dimension=0, tiled=True
            ).astype(jnp.float32),
            lax.psum_scatter(
                out_grad.astype(jnp.bfloat16), "shard", scatter_dimension=0, tiled=True
            ).astype(jnp.float32),
            lax.psum_scatter(
                gate_up_grad.astype(jnp.bfloat16), "shard", scatter_dimension=0, tiled=True
            ).astype(jnp.float32),
            lax.psum_scatter(
                down_grad.astype(jnp.bfloat16), "shard", scatter_dimension=1, tiled=True
            ).astype(jnp.float32),
            lax.psum_scatter(
                gains_grad.astype(jnp.bfloat16), "shard", scatter_dimension=1, tiled=True
            ).astype(jnp.float32),
        )
        qkv_red, out_red, gains_red = (
            lax.psum(qkv_part.astype(jnp.bfloat16), ("context", "tensor")).astype(jnp.float32),
            lax.psum(out_part.astype(jnp.bfloat16), ("context", "tensor")).astype(jnp.float32),
            lax.psum(gains_part.astype(jnp.bfloat16), ("context", "tensor")).astype(jnp.float32),
        )
        gate_up_red, down_red = (
            lax.psum(gate_up_part.astype(jnp.bfloat16), "context").astype(jnp.float32),
            lax.psum(down_part.astype(jnp.bfloat16), "context").astype(jnp.float32),
        )
    results = adam_step(qkv_weight, qkv_first, qkv_second, qkv_red, RATES[0], DECAYS[0])
    results = results + adam_step(out_weight, out_first, out_second, out_red, RATES[1], DECAYS[1])
    results = results + adam_step(
        gate_up_weight, gate_up_first, gate_up_second, gate_up_red, RATES[2], DECAYS[2]
    )
    results = results + adam_step(
        down_weight, down_first, down_second, down_red, RATES[3], DECAYS[3]
    )
    results = results + adam_step(
        norm_gains, gains_first, gains_second, gains_red, RATES[4], DECAYS[4]
    )
    return (block_out, tokens_grad) + results


def solution(mesh):
    placed = (
        P(("shard", "context", "tensor"), None),
        P(("shard", "context", "tensor"), None),
        P("shard", None),
        P("shard", None),
        P("shard", None),
        P("shard", None),
        P("shard", None),
        P("shard", None),
        P("shard", None),
        P("shard", None, "tensor"),
        P("shard", None, "tensor"),
        P("shard", None, "tensor"),
        P("tensor", "shard"),
        P("tensor", "shard"),
        P("tensor", "shard"),
        P(None, "shard"),
        P(None, "shard"),
        P(None, "shard"),
    )
    return jax.shard_map(
        shards,
        mesh=mesh,
        in_specs=placed,
        out_specs=(
            P(("shard", "context", "tensor"), None),
            P(("shard", "context", "tensor"), None),
            P("shard", None),
            P("shard", None),
            P("shard", None),
            P("shard", None),
            P("shard", None),
            P("shard", None),
            P("shard", None, "tensor"),
            P("shard", None, "tensor"),
            P("shard", None, "tensor"),
            P("tensor", "shard"),
            P("tensor", "shard"),
            P("tensor", "shard"),
            P(None, "shard"),
            P(None, "shard"),
            P(None, "shard"),
        ),
        check_vma=False,
    )
```

```python
import functools
import math

import jax
import jax.numpy as jnp
from jax import lax
from jax.experimental import pallas as pl
from jax.experimental.pallas import tpu as pltpu
from jax.sharding import PartitionSpec as P

MODEL_WIDTH = 960
QUERY_HEADS = 15
KEY_VALUE_HEADS = 5
HEAD_SIZE = 64
STEP = 10
KEY_COLUMNS = 320


NEGATIVE_HUGE = -1e30
NORM_EPS = 1e-05
ROPE_BASE = 100000.0
BETA_ONE = 0.9
BETA_TWO = 0.95
ADAM_EPS = 1e-08
RATES = (0.06, 1.0, 0.06, 0.04, 0.4)
DECAYS = (0.1, 0.1, 0.1, 0.1, 0.0)


MESH = pl.DeviceIdType.MESH
BF16 = jnp.bfloat16
GAIN_ROWS = 16
ROW_TILE = 16
ATTN_CHUNKS = 4
FFN_CHUNKS = 3


def plane_peers():
    s = lax.axis_index("shard")
    c = lax.axis_index("context")
    t = lax.axis_index("tensor")
    x, y = lax.rem(s, 2), s // 2
    across, along, diagonal = 2 * y + 1 - x, 2 * (1 - y) + x, 2 * (1 - y) + 1 - x
    return s, c, t, across, along, diagonal


def greet(devices):
    barrier = pltpu.get_barrier_semaphore()
    for device in devices:
        pl.semaphore_signal(barrier, inc=1, device_id=device, device_id_type=MESH)
    pl.semaphore_wait(barrier, len(devices))


def gather_kernel(w, gains, out, gains_out, send, recv, local):
    s, c, t, across, along, diagonal = plane_peers()
    to_x, to_y, to_d, to_core = (across, c, t), (along, c, t), (diagonal, c, t), (s, c, 1 - t)
    greet((to_x, to_y, to_d, to_core))
    rows = w.shape[1]
    upper = (rows // 2 + ROW_TILE - 1) // ROW_TILE * ROW_TILE
    parts = (pl.ds(0, upper), pl.ds(upper, rows - upper))

    def copy(src, dst, lane, k, device):
        return pltpu.make_async_remote_copy(
            src_ref=src,
            dst_ref=dst,
            send_sem=send.at[lane, k],
            recv_sem=recv.at[lane, k],
            device_id=device,
            device_id_type=MESH,
        )

    def own(lane, k):
        return copy(w.at[t, parts[k]], out.at[t, s, parts[k]], lane, k, (to_x, to_y)[lane])

    def onward(k):
        place = out.at[t, (across, along)[k], parts[k]]
        return copy(place, place, 2, k, (to_y, to_x)[k])

    def sideways(i, k):
        place = out.at[t, (across, along, diagonal)[i], parts[k]]
        return copy(place, place, 3 + i, k, to_core)

    def small(i):
        return copy(gains, gains_out.at[s], 6, i, (to_x, to_y, to_d)[i])

    keep = pltpu.make_async_copy(w, out.at[:, s], local.at[0])
    keep_gains = pltpu.make_async_copy(gains, gains_out.at[s], local.at[1])
    for k in range(2):
        own(0, k).start()
        own(1, 1 - k).start()
    for i in range(3):
        small(i).start()
    keep.start()
    keep_gains.start()
    own(0, 0).wait_recv()
    onward(0).start()
    own(1, 1).wait_recv()
    onward(1).start()
    sideways(0, 0).start()
    sideways(1, 1).start()
    own(0, 1).wait_recv()
    sideways(0, 1).start()
    own(1, 0).wait_recv()
    sideways(1, 0).start()
    for k in range(2):
        onward(k).wait_recv()
        sideways(2, k).start()
    for i in range(3):
        for k in range(2):
            sideways(i, k).wait()
        small(i).wait()
    for k in range(2):
        own(0, k).wait_send()
        own(1, k).wait_send()
        onward(k).wait_send()
    keep.wait()
    keep_gains.wait()


def gather_weights(w, gains):
    blocks, rows, cols = w.shape
    return pl.pallas_call(
        gather_kernel,
        out_shape=(
            jax.ShapeDtypeStruct((blocks, 4, rows, cols), BF16),
            jax.ShapeDtypeStruct((4,) + gains.shape, BF16),
        ),
        in_specs=[pl.BlockSpec(memory_space=pl.ANY)] * 2,
        out_specs=[pl.BlockSpec(memory_space=pl.ANY)] * 2,
        scratch_shapes=[
            pltpu.SemaphoreType.DMA((7, 3)),
            pltpu.SemaphoreType.DMA((7, 3)),
            pltpu.SemaphoreType.DMA((2,)),
        ],
        compiler_params=pltpu.CompilerParams(collective_id=0, has_side_effects=True),
        name="gather_weights",
    )(w, gains)


ACROSS = ((0, 1), (1, 0), (2, 3), (3, 2))
ALONG = ((0, 2), (2, 0), (1, 3), (3, 1))


def swap(block, pairs):
    return lax.ppermute(block, "shard", pairs)


def plane_gather(block, x_first):
    s, c, t, across, along, diagonal = plane_peers()
    from_x, from_y = swap(block, ACROSS), swap(block, ALONG)
    from_d = swap(from_x, ALONG) if x_first else swap(from_y, ACROSS)
    whole = jnp.zeros((4,) + block.shape, block.dtype)
    for owner, part in ((s, block), (across, from_x), (along, from_y), (diagonal, from_d)):
        whole = lax.dynamic_update_index_in_dim(whole, part, owner, 0)
    return whole


def plane_scatter(blocks, x_first):
    s, c, t, across, along, diagonal = plane_peers()
    near, far, straight, turn = (across, along, ACROSS, ALONG) if x_first else (along, across, ALONG, ACROSS)

    def part(owner):
        return lax.dynamic_index_in_dim(blocks, owner, 0, keepdims=False)

    first = swap(part(diagonal), straight)
    direct = swap(part(near), straight)
    summed = swap((part(far).astype(jnp.float32) + first.astype(jnp.float32)).astype(BF16), turn)
    total = part(s).astype(jnp.float32) + direct.astype(jnp.float32) + summed.astype(jnp.float32)
    return total.astype(BF16)


def reduce_kernel(
    n, chunks, attn, ffn, attn_out, ffn_out, side, first, partial, direct, summed, line, middle, carry, send, recv
):
    s, c, t, across, along, diagonal = plane_peers()
    half = n // 2
    inner = jnp.where(c < half, c + 1, c - 1)
    outer = jnp.where(c < half, c - 1, c + 1)
    to_x, to_y, to_core = (across, c, t), (along, c, t), (s, c, 1 - t)
    at_end = (c == 0) | (c == n - 1)
    at_middle = (c == half - 1) | (c == half)
    barrier = pltpu.get_barrier_semaphore()
    for device in (to_x, to_y, to_core, (s, inner, t)):
        pl.semaphore_signal(barrier, inc=1, device_id=device, device_id_type=MESH)

    @pl.when(jnp.logical_not(at_end))
    def _():
        pl.semaphore_signal(barrier, inc=1, device_id=(s, outer, t), device_id_type=MESH)
        pl.semaphore_wait(barrier, 5)

    @pl.when(at_end)
    def _():
        pl.semaphore_wait(barrier, 4)

    def copy(src, dst, lane, i, device):
        return pltpu.make_async_remote_copy(
            src_ref=src,
            dst_ref=dst,
            send_sem=send.at[lane, i],
            recv_sem=recv.at[lane, i],
            device_id=device,
            device_id_type=MESH,
        )

    count = len(chunks)
    attn_chunks = [i for i in range(count) if chunks[i][0] == 0]
    base = attn_chunks[0]

    def rows_of(i, buffer):
        return buffer.at[i, pl.ds(0, chunks[i][2])]

    def plane_rows(i, buffer):
        return buffer.at[i - base, pl.ds(0, chunks[i][2])]

    def mine(i, owner):
        k, start, size = chunks[i]
        return side.at[owner, pl.ds(start, size)]

    def result(i):
        k, start, size = chunks[i]
        if k == 0:
            return attn_out.at[t, pl.ds(start, size)]
        return ffn_out.at[k - 1, pl.ds(start, size)]

    def addend(i):
        k, start, size = chunks[i]
        return rows_of(i, carry) if k == 0 else ffn.at[k - 1, pl.ds(start, size)]

    def x_first(i):
        return (i - base) % 2 == 0

    def add(*refs):
        total = refs[0][...].astype(jnp.float32)
        for ref in refs[1:]:
            total = total + ref[...].astype(jnp.float32)
        return total.astype(BF16)

    def send_first(i):
        return copy(mine(i, diagonal), plane_rows(i, first), 0, i, to_x if x_first(i) else to_y)

    def send_direct(i):
        owner, device = (across, to_x) if x_first(i) else (along, to_y)
        return copy(mine(i, owner), plane_rows(i, direct), 1, i, device)

    def send_summed(i):
        return copy(plane_rows(i, partial), plane_rows(i, summed), 2, i, to_y if x_first(i) else to_x)

    def send_in(i):
        return copy(addend(i), rows_of(i, line), 3, i, (s, inner, t))

    def send_through(i):
        return copy(rows_of(i, carry), rows_of(i, line), 3, i, (s, inner, t))

    def send_middle(i):
        return copy(rows_of(i, carry), rows_of(i, middle), 4, i, (s, inner, t))

    def send_out(i):
        return copy(result(i), result(i), 5, i, (s, outer, t))

    def send_core(i):
        return copy(result(i), result(i), 6, i, to_core)

    def send_side():
        return copy(attn.at[1 - t], side, 7, 0, to_core)

    def start_in(i):
        @pl.when(at_end)
        def _():
            send_in(i).start()

    def stage_cores():
        send_side().wait()
        for owner in range(4):
            side[owner] = add(attn.at[t, owner], side.at[owner])
        for i in attn_chunks:
            send_first(i).start()
        for i in attn_chunks:
            send_direct(i).start()

    def stage_plane(i):
        send_first(i).wait_recv()
        owner = along if x_first(i) else across
        partial[i - base, pl.ds(0, chunks[i][2])] = add(mine(i, owner), plane_rows(i, first))
        send_summed(i).start()

    def stage_chips(i):
        send_direct(i).wait_recv()
        send_summed(i).wait_recv()
        carry[i, pl.ds(0, chunks[i][2])] = add(mine(i, s), plane_rows(i, direct), plane_rows(i, summed))
        start_in(i)

    def stage_fold(i):
        @pl.when(jnp.logical_not(at_end))
        def _():
            send_in(i).wait_recv()
            carry[i, pl.ds(0, chunks[i][2])] = add(addend(i), rows_of(i, line))

            @pl.when(at_middle)
            def _():
                send_middle(i).start()

            @pl.when(jnp.logical_not(at_middle))
            def _():
                send_through(i).start()

    def stage_total(i):
        @pl.when(at_middle)
        def _():
            send_middle(i).wait()
            result(i)[...] = add(rows_of(i, carry), rows_of(i, middle))

        @pl.when(jnp.logical_not(at_middle))
        def _():
            send_out(i).wait_recv()
            send_in(i).wait_send()

        @pl.when(jnp.logical_not(at_end))
        def _():
            send_out(i).start()

        if chunks[i][0] == 0:
            send_core(i).start()

    send_side().start()
    for i in range(base):
        start_in(i)
    for step in range(count + 1):
        if step == 2:
            stage_cores()
        if step == 4:
            for i in attn_chunks:
                stage_plane(i)
        if 6 <= step < 6 + len(attn_chunks):
            stage_chips(attn_chunks[step - 6])
        if step < count:
            stage_fold(step)
        if step >= 1:
            stage_total(step - 1)
    for i in range(count):
        if chunks[i][0] == 0:
            send_first(i).wait_send()
            send_direct(i).wait_send()
            send_summed(i).wait_send()
            send_core(i).wait()

        @pl.when(jnp.logical_not(at_end))
        def _():
            send_out(i).wait_send()


def reduce_grads(n, attn, ffn):
    attn_rows, ffn_rows, cols = attn.shape[2], ffn.shape[1], attn.shape[3]
    chunks = []
    for k in (1, 2, 3, 0):
        rows, pieces = (attn_rows, ATTN_CHUNKS) if k == 0 else (ffn_rows, FFN_CHUNKS)
        for j in range(pieces):
            chunks.append((k, j * (rows // pieces), rows // pieces))
    count, most = len(chunks), max(size for k, start, size in chunks)
    held = pltpu.VMEM((count, most, cols), BF16)
    plane_held = pltpu.VMEM((ATTN_CHUNKS, most, cols), BF16)
    return pl.pallas_call(
        functools.partial(reduce_kernel, n, tuple(chunks)),
        out_shape=(
            jax.ShapeDtypeStruct((2, attn_rows, cols), BF16),
            jax.ShapeDtypeStruct((3, ffn_rows, cols), BF16),
        ),
        in_specs=[pl.BlockSpec(memory_space=pltpu.VMEM)] * 2,
        out_specs=[pl.BlockSpec(memory_space=pltpu.VMEM)] * 2,
        scratch_shapes=[pltpu.VMEM((4, attn_rows, cols), BF16)]
        + [plane_held] * 4
        + [held] * 3
        + [pltpu.SemaphoreType.DMA((8, count)), pltpu.SemaphoreType.DMA((8, count))],
        compiler_params=pltpu.CompilerParams(
            collective_id=1, has_side_effects=True, vmem_limit_bytes=48 * 1024 * 1024
        ),
        name="reduce_grads",
    )(attn, ffn)


def rope_angles(position):
    halfway = HEAD_SIZE // 2
    frequency = jnp.exp(
        jnp.arange(halfway, dtype=jnp.float32) * (-2.0 * math.log(ROPE_BASE) / HEAD_SIZE)
    )
    angles = position.astype(jnp.float32)[:, None] * frequency[None, :]
    return (jnp.cos(angles)[:, None, :], jnp.sin(angles)[:, None, :])


def apply_rotary(vectors, cosine_table, sine_table):
    halfway = HEAD_SIZE // 2
    leading = vectors[..., :halfway]
    trailing = vectors[..., halfway:]
    return jnp.concatenate(
        [
            leading * cosine_table - trailing * sine_table,
            trailing * cosine_table + leading * sine_table,
        ],
        axis=-1,
    )


def unrotate(gradient, cosine_table, sine_table):
    halfway = HEAD_SIZE // 2
    leading = gradient[..., :halfway]
    trailing = gradient[..., halfway:]
    return jnp.concatenate(
        [
            leading * cosine_table + trailing * sine_table,
            trailing * cosine_table - leading * sine_table,
        ],
        axis=-1,
    )


def doc_starts(length_row, row_index):
    doc_ends = jnp.cumsum(length_row)
    before = jnp.where(doc_ends[None, :] <= row_index[:, None], length_row[None, :], 0)
    return jnp.sum(before, axis=1)


def rms_norm(values, gain_row):
    inverse = lax.rsqrt(jnp.mean(values * values, axis=-1, keepdims=True) + NORM_EPS)
    return (values * inverse * gain_row, inverse)


def norm_back(values, inverse, gain_row, gradient):
    unit_values = values * inverse
    scaled = gradient * gain_row
    gain_grad = jnp.sum(gradient * unit_values, axis=0)
    values_grad = inverse * (
        scaled - unit_values * jnp.mean(scaled * unit_values, axis=-1, keepdims=True)
    )
    return (gain_grad, values_grad)


def adam_step(weight, moment_one, moment_two, gradient, learning, decay_rate):
    first_new = BETA_ONE * moment_one + (1.0 - BETA_ONE) * gradient
    second_new = BETA_TWO * moment_two + (1.0 - BETA_TWO) * gradient * gradient
    first_hat = first_new / (1.0 - BETA_ONE**STEP)
    second_hat = second_new / (1.0 - BETA_TWO**STEP)
    weight_new = weight - learning * (
        first_hat / (jnp.sqrt(second_hat) + ADAM_EPS) + decay_rate * weight
    )
    return (weight_new, first_new, second_new)


def block_scores(query_low, key_block, row_index, row_start, block_id):
    rows_per_block = key_block.shape[0]
    scores = jnp.einsum(
        "qhgd,khd->qhgk", query_low, key_block, preferred_element_type=jnp.float32
    ) * (1.0 / math.sqrt(HEAD_SIZE))
    column_index = block_id * rows_per_block + jnp.arange(rows_per_block, dtype=jnp.int32)
    visible = (column_index[None, :] >= row_start[:, None]) & (
        column_index[None, :] <= row_index[:, None]
    )
    return (scores, visible[:, None, None, :])


def shards(
    tokens,
    cotangent,
    lengths,
    qkv_weight,
    qkv_first,
    qkv_second,
    out_weight,
    out_first,
    out_second,
    gate_up_weight,
    gate_up_first,
    gate_up_second,
    down_weight,
    down_first,
    down_second,
    norm_gains,
    gains_first,
    gains_second,
):
    shard_rows = tokens.shape[0]
    pack_groups = QUERY_HEADS // KEY_VALUE_HEADS
    qkv_low = qkv_weight.astype(jnp.bfloat16)
    out_low = out_weight.astype(jnp.bfloat16)
    gate_up_low = gate_up_weight.astype(jnp.bfloat16)
    down_low = down_weight.astype(jnp.bfloat16)
    gains_low = norm_gains.astype(jnp.bfloat16)
    plane = lax.axis_size("shard") == 4 and lax.axis_size("context") % 2 == 0
    width, hidden_units = MODEL_WIDTH + KEY_COLUMNS, down_weight.shape[0]
    plane = plane and hidden_units == width
    if plane:
        weights = jnp.stack(
            [qkv_low[:, :width], jnp.concatenate([qkv_low[:, width:], out_low], axis=1)]
        )
        own_gains = jnp.pad(gains_low, ((0, GAIN_ROWS - 2), (0, 0)))
        gathered, gains_parts = gather_weights(weights, own_gains)
        gathered, gains_parts, gate_low, up_low, down_low_t = lax.optimization_barrier(
            (gathered, gains_parts, gate_up_low[:, 0], gate_up_low[:, 1], down_low.T)
        )
        gathered = gathered.reshape(2, MODEL_WIDTH, width)
        qkv_mat = jnp.concatenate([gathered[0], gathered[1, :, :KEY_COLUMNS]], axis=1)
        out_mat = gathered[1, :, KEY_COLUMNS:]
        gate_mat = plane_gather(gate_low, True).reshape(MODEL_WIDTH, hidden_units)
        up_mat = plane_gather(up_low, False).reshape(MODEL_WIDTH, hidden_units)
        middle_column = hidden_units // 2
        down_mat_t = jnp.concatenate(
            [
                plane_gather(down_low_t[:, :middle_column], True),
                plane_gather(down_low_t[:, middle_column:], False),
            ],
            axis=2,
        ).reshape(MODEL_WIDTH, hidden_units)
        gains_all = gains_parts[:, :2].transpose(1, 0, 2).reshape(2, MODEL_WIDTH)
    else:
        qkv_mat = lax.all_gather(qkv_low, "shard", axis=0, tiled=True)
        out_mat = lax.all_gather(out_low, "shard", axis=0, tiled=True)
        gate_up_mat = lax.all_gather(gate_up_low, "shard", axis=0, tiled=True)
        gate_mat, up_mat = gate_up_mat[:, 0], gate_up_mat[:, 1]
        down_mat_t = lax.all_gather(down_low, "shard", axis=1, tiled=True).T
        gains_all = lax.all_gather(gains_low, "shard", axis=1, tiled=True)
    gains_full = gains_all.astype(jnp.float32)
    tensor_size = lax.axis_size("tensor")
    offset = (lax.axis_index("context") * tensor_size + lax.axis_index("tensor")) * shard_rows
    row_index = offset + jnp.arange(shard_rows, dtype=jnp.int32)
    row_start = doc_starts(lengths[0], row_index)
    cosine_table, sine_table = rope_angles(row_index - row_start)
    inputs = tokens.astype(jnp.float32)
    normed_one, inverse_one = rms_norm(inputs, gains_full[0])
    first_low = normed_one.astype(jnp.bfloat16)
    projected_output = jnp.dot(first_low, qkv_mat, preferred_element_type=jnp.float32)
    query_low = (
        apply_rotary(
            projected_output[:, :MODEL_WIDTH].reshape(shard_rows, QUERY_HEADS, HEAD_SIZE),
            cosine_table,
            sine_table,
        )
        .astype(jnp.bfloat16)
        .reshape(shard_rows, KEY_VALUE_HEADS, pack_groups, HEAD_SIZE)
    )
    keys_low = (
        apply_rotary(
            projected_output[:, MODEL_WIDTH : MODEL_WIDTH + KEY_COLUMNS].reshape(
                shard_rows, KEY_VALUE_HEADS, HEAD_SIZE
            ),
            cosine_table,
            sine_table,
        )
        .astype(jnp.bfloat16)
        .reshape(shard_rows, KEY_COLUMNS)
    )
    kv_local = jnp.concatenate(
        [keys_low, projected_output[:, MODEL_WIDTH + KEY_COLUMNS :].astype(jnp.bfloat16)], axis=1
    )
    key_value_whole = lax.all_gather(kv_local, ("context", "tensor"), axis=0, tiled=True)
    total_keys = key_value_whole.shape[0]
    rows_per_block = min(512, total_keys)
    count_of_blocks = total_keys // rows_per_block
    key_value_blocks = key_value_whole.reshape(
        count_of_blocks, rows_per_block, 2, KEY_VALUE_HEADS, HEAD_SIZE
    )
    block_numbers = jnp.arange(count_of_blocks, dtype=jnp.int32)

    def scan_total(scan_carry, scan_item):
        running, running_sum = scan_carry
        block_id, kv_block = scan_item
        scores, visible = block_scores(query_low, kv_block[:, 0], row_index, row_start, block_id)
        masked = jnp.where(visible, scores, NEGATIVE_HUGE)
        highest = jnp.maximum(running, jnp.max(masked, axis=-1))
        exponent = jnp.where(visible, jnp.exp(masked - highest[..., None]), 0.0)
        running_sum = running_sum * jnp.exp(running - highest) + jnp.sum(exponent, axis=-1)
        return ((highest, running_sum), None)

    latest_start = jnp.full((shard_rows, KEY_VALUE_HEADS, pack_groups), NEGATIVE_HUGE, jnp.float32)
    (running, running_sum), unused = lax.scan(
        scan_total, (latest_start, jnp.zeros_like(latest_start)), (block_numbers, key_value_blocks)
    )
    log_total = running + jnp.log(running_sum)

    def sweep_output(accumulated, scan_item):
        block_id, kv_block = scan_item
        scores, visible = block_scores(query_low, kv_block[:, 0], row_index, row_start, block_id)
        softmax_rows = jnp.where(visible, jnp.exp(scores - log_total[..., None]), 0.0)
        accumulated = accumulated + jnp.einsum(
            "qhgk,khd->qhgd",
            softmax_rows.astype(jnp.bfloat16),
            kv_block[:, 1],
            preferred_element_type=jnp.float32,
        )
        return (accumulated, None)

    attended_heads, unused = lax.scan(
        sweep_output,
        jnp.zeros((shard_rows, KEY_VALUE_HEADS, pack_groups, HEAD_SIZE), jnp.float32),
        (block_numbers, key_value_blocks),
    )
    attended_low = attended_heads.reshape(shard_rows, MODEL_WIDTH).astype(jnp.bfloat16)
    branch = jnp.dot(attended_low, out_mat, preferred_element_type=jnp.float32)
    hidden_state = inputs + branch
    normed_two, inverse_two = rms_norm(hidden_state, gains_full[1])
    second_low = normed_two.astype(jnp.bfloat16)
    ffn_rows = lax.all_gather(second_low, "tensor", axis=0, tiled=True)
    gate_vals = jnp.dot(ffn_rows, gate_mat, preferred_element_type=jnp.float32)
    upward = jnp.dot(ffn_rows, up_mat, preferred_element_type=jnp.float32)
    gate_sigmoid = jax.nn.sigmoid(gate_vals)
    activated = gate_vals * gate_sigmoid
    hidden_low = (activated * upward).astype(jnp.bfloat16)
    partial_out = jnp.einsum("tf,df->td", hidden_low, down_mat_t, preferred_element_type=jnp.float32)
    ffn_out = lax.psum_scatter(
        partial_out.astype(jnp.bfloat16), "tensor", scatter_dimension=0, tiled=True
    ).astype(jnp.float32)
    block_out = (hidden_state + ffn_out).astype(jnp.bfloat16)
    grad_rows = lax.all_gather(cotangent, "tensor", axis=0, tiled=True)
    down_grad_t = jnp.einsum("td,tf->df", grad_rows, hidden_low, preferred_element_type=jnp.float32)
    hidden_grad = jnp.dot(grad_rows, down_mat_t, preferred_element_type=jnp.float32)
    gate_grad = hidden_grad * upward * gate_sigmoid * (1.0 + gate_vals * (1.0 - gate_sigmoid))
    upward_grad = hidden_grad * activated
    gate_grad_low = gate_grad.astype(jnp.bfloat16)
    upward_grad_low = upward_grad.astype(jnp.bfloat16)
    gate_grad = jnp.einsum("td,tf->df", ffn_rows, gate_grad_low, preferred_element_type=jnp.float32)
    upward_grad = jnp.einsum(
        "td,tf->df", ffn_rows, upward_grad_low, preferred_element_type=jnp.float32
    )
    normed_part = jnp.einsum(
        "tf,df->td", gate_grad_low, gate_mat, preferred_element_type=jnp.float32
    ) + jnp.einsum("tf,df->td", upward_grad_low, up_mat, preferred_element_type=jnp.float32)
    normed_two_grad = lax.psum_scatter(
        normed_part.astype(jnp.bfloat16), "tensor", scatter_dimension=0, tiled=True
    ).astype(jnp.float32)
    gain_two_grad, state_norm_grad = norm_back(
        hidden_state, inverse_two, gains_full[1], normed_two_grad
    )
    state_grad = cotangent.astype(jnp.float32) + state_norm_grad
    branch_low = state_grad.astype(jnp.bfloat16)
    out_grad = jnp.einsum("tk,td->kd", attended_low, branch_low, preferred_element_type=jnp.float32)
    attended_gradient = jnp.einsum(
        "td,kd->tk", branch_low, out_mat, preferred_element_type=jnp.float32
    )
    attended_gradient_narrow = attended_gradient.astype(jnp.bfloat16).reshape(
        shard_rows, KEY_VALUE_HEADS, pack_groups, HEAD_SIZE
    )
    delta_rows = jnp.sum(attended_gradient_narrow.astype(jnp.float32) * attended_heads, axis=-1)

    def sweep_backward(query_grad, scan_item):
        block_id, kv_block = scan_item
        scores, visible = block_scores(query_low, kv_block[:, 0], row_index, row_start, block_id)
        softmax_rows = jnp.where(visible, jnp.exp(scores - log_total[..., None]), 0.0)
        softmax_low = softmax_rows.astype(jnp.bfloat16)
        probs_grad = jnp.einsum(
            "qhgd,khd->qhgk",
            attended_gradient_narrow,
            kv_block[:, 1],
            preferred_element_type=jnp.float32,
        )
        scores_low = (softmax_rows * (probs_grad - delta_rows[..., None])).astype(jnp.bfloat16)
        query_grad = query_grad + jnp.einsum(
            "qhgk,khd->qhgd", scores_low, kv_block[:, 0], preferred_element_type=jnp.float32
        ) * (1.0 / math.sqrt(HEAD_SIZE))
        key_grad = jnp.einsum(
            "qhgk,qhgd->khd", scores_low, query_low, preferred_element_type=jnp.float32
        ) * (1.0 / math.sqrt(HEAD_SIZE))
        value_grad = jnp.einsum(
            "qhgk,qhgd->khd",
            softmax_low,
            attended_gradient_narrow,
            preferred_element_type=jnp.float32,
        )
        return (query_grad, jnp.stack([key_grad, value_grad], axis=1))

    query_grad, kv_terms = lax.scan(
        sweep_backward,
        jnp.zeros((shard_rows, KEY_VALUE_HEADS, pack_groups, HEAD_SIZE), jnp.float32),
        (block_numbers, key_value_blocks),
    )
    kv_terms = kv_terms.reshape(total_keys, 2 * KEY_COLUMNS)
    key_value_gradient = lax.psum_scatter(
        kv_terms.astype(jnp.bfloat16), ("context", "tensor"), scatter_dimension=0, tiled=True
    ).astype(jnp.float32)
    key_back = unrotate(
        key_value_gradient[:, :KEY_COLUMNS].reshape(shard_rows, KEY_VALUE_HEADS, HEAD_SIZE),
        cosine_table,
        sine_table,
    ).reshape(shard_rows, KEY_COLUMNS)
    query_back = unrotate(
        query_grad.reshape(shard_rows, QUERY_HEADS, HEAD_SIZE), cosine_table, sine_table
    ).reshape(shard_rows, MODEL_WIDTH)
    projected_low = jnp.concatenate(
        [query_back, key_back, key_value_gradient[:, KEY_COLUMNS:]], axis=1
    ).astype(jnp.bfloat16)
    qkv_grad = jnp.einsum("td,tk->dk", first_low, projected_low, preferred_element_type=jnp.float32)
    normed_one_grad = jnp.einsum(
        "tk,dk->td", projected_low, qkv_mat, preferred_element_type=jnp.float32
    )
    gain_one_grad, input_norm_grad = norm_back(inputs, inverse_one, gains_full[0], normed_one_grad)
    tokens_grad = state_grad + input_norm_grad
    gains_grad = jnp.stack([gain_one_grad, gain_two_grad])
    if plane:
        rows = MODEL_WIDTH // 4
        attn_grad = jnp.stack(
            [
                qkv_grad[:, :width].astype(jnp.bfloat16),
                jnp.concatenate([qkv_grad[:, width:], out_grad], axis=1).astype(jnp.bfloat16),
            ]
        ).reshape(2, 4, rows, width)
        gain_rows = jnp.pad(
            gains_grad.astype(jnp.bfloat16).reshape(2, 4, rows).transpose(1, 0, 2),
            ((0, 0), (0, GAIN_ROWS - 2), (0, width - rows)),
        )
        gain_rows = jnp.stack([gain_rows, jnp.zeros_like(gain_rows)])
        attn_grad = jnp.concatenate([attn_grad, gain_rows], axis=2)
        gate_blocks, up_blocks, down_blocks = (
            part.astype(jnp.bfloat16).reshape(4, rows, width)
            for part in (gate_grad, upward_grad, down_grad_t)
        )
        down_part = jnp.concatenate(
            [
                plane_scatter(down_blocks[:, :, :middle_column], True),
                plane_scatter(down_blocks[:, :, middle_column:], False),
            ],
            axis=1,
        )
        ffn_grad = jnp.stack(
            [plane_scatter(gate_blocks, True), plane_scatter(up_blocks, False), down_part]
        )
        attn_red, ffn_red = reduce_grads(lax.axis_size("context"), attn_grad, ffn_grad)
        gains_red = attn_red[0, rows : rows + 2, :rows].astype(jnp.float32)
        qkv_red = jnp.concatenate(
            [attn_red[0, :rows], attn_red[1, :rows, :KEY_COLUMNS]], axis=1
        ).astype(jnp.float32)
        out_red = attn_red[1, :rows, KEY_COLUMNS:].astype(jnp.float32)
        gate_up_red = jnp.stack([ffn_red[0], ffn_red[1]], axis=1).astype(jnp.float32)
        down_red = ffn_red[2].T.astype(jnp.float32)
    else:
        gate_up_grad = jnp.stack([gate_grad, upward_grad], axis=1)
        down_grad = down_grad_t.T
        qkv_part, out_part, gate_up_part, down_part, gains_part = (
            lax.psum_scatter(
                qkv_grad.astype(jnp.bfloat16), "shard", scatter_dimension=0, tiled=True
            ).astype(jnp.float32),
            lax.psum_scatter(
                out_grad.astype(jnp.bfloat16), "shard", scatter_dimension=0, tiled=True
            ).astype(jnp.float32),
            lax.psum_scatter(
                gate_up_grad.astype(jnp.bfloat16), "shard", scatter_dimension=0, tiled=True
            ).astype(jnp.float32),
            lax.psum_scatter(
                down_grad.astype(jnp.bfloat16), "shard", scatter_dimension=1, tiled=True
            ).astype(jnp.float32),
            lax.psum_scatter(
                gains_grad.astype(jnp.bfloat16), "shard", scatter_dimension=1, tiled=True
            ).astype(jnp.float32),
        )
        qkv_red, out_red, gains_red = (
            lax.psum(qkv_part.astype(jnp.bfloat16), ("context", "tensor")).astype(jnp.float32),
            lax.psum(out_part.astype(jnp.bfloat16), ("context", "tensor")).astype(jnp.float32),
            lax.psum(gains_part.astype(jnp.bfloat16), ("context", "tensor")).astype(jnp.float32),
        )
        gate_up_red, down_red = (
            lax.psum(gate_up_part.astype(jnp.bfloat16), "context").astype(jnp.float32),
            lax.psum(down_part.astype(jnp.bfloat16), "context").astype(jnp.float32),
        )
    results = adam_step(qkv_weight, qkv_first, qkv_second, qkv_red, RATES[0], DECAYS[0])
    results = results + adam_step(out_weight, out_first, out_second, out_red, RATES[1], DECAYS[1])
    results = results + adam_step(
        gate_up_weight, gate_up_first, gate_up_second, gate_up_red, RATES[2], DECAYS[2]
    )
    results = results + adam_step(
        down_weight, down_first, down_second, down_red, RATES[3], DECAYS[3]
    )
    results = results + adam_step(
        norm_gains, gains_first, gains_second, gains_red, RATES[4], DECAYS[4]
    )
    return (block_out, tokens_grad) + results


def solution(mesh):
    placed = (
        P(("shard", "context", "tensor"), None),
        P(("shard", "context", "tensor"), None),
        P("shard", None),
        P("shard", None),
        P("shard", None),
        P("shard", None),
        P("shard", None),
        P("shard", None),
        P("shard", None),
        P("shard", None, "tensor"),
        P("shard", None, "tensor"),
        P("shard", None, "tensor"),
        P("tensor", "shard"),
        P("tensor", "shard"),
        P("tensor", "shard"),
        P(None, "shard"),
        P(None, "shard"),
        P(None, "shard"),
    )
    return jax.shard_map(
        shards,
        mesh=mesh,
        in_specs=placed,
        out_specs=(
            P(("shard", "context", "tensor"), None),
            P(("shard", "context", "tensor"), None),
            P("shard", None),
            P("shard", None),
            P("shard", None),
            P("shard", None),
            P("shard", None),
            P("shard", None),
            P("shard", None, "tensor"),
            P("shard", None, "tensor"),
            P("shard", None, "tensor"),
            P("tensor", "shard"),
            P("tensor", "shard"),
            P("tensor", "shard"),
            P(None, "shard"),
            P(None, "shard"),
            P(None, "shard"),
        ),
        check_vma=False,
    )
```

```python
import functools
import math

import jax
import jax.numpy as jnp
from jax import lax
from jax.experimental import pallas as pl
from jax.experimental.pallas import tpu as pltpu
from jax.sharding import PartitionSpec as P

MODEL_WIDTH = 960
QUERY_HEADS = 15
KEY_VALUE_HEADS = 5
HEAD_SIZE = 64
STEP = 10
KEY_COLUMNS = 320


NORM_EPS = 1e-05
ROPE_BASE = 100000.0
BETA_ONE = 0.9
BETA_TWO = 0.95
ADAM_EPS = 1e-08
RATES = (0.06, 1.0, 0.06, 0.04, 0.4)
DECAYS = (0.1, 0.1, 0.1, 0.1, 0.0)


MESH = pl.DeviceIdType.MESH
BF16 = jnp.bfloat16
NEGATIVE_HUGE = -1e30
GAIN_ROWS = 16
ROW_TILE = 16
ATTN_CHUNKS = 4
FFN_CHUNKS = 3


def plane_peers():
    s = lax.axis_index("shard")
    c = lax.axis_index("context")
    t = lax.axis_index("tensor")
    x, y = lax.rem(s, 2), s // 2
    across, along, diagonal = 2 * y + 1 - x, 2 * (1 - y) + x, 2 * (1 - y) + 1 - x
    return s, c, t, across, along, diagonal


def greet(devices):
    barrier = pltpu.get_barrier_semaphore()
    for device in devices:
        pl.semaphore_signal(barrier, inc=1, device_id=device, device_id_type=MESH)
    pl.semaphore_wait(barrier, len(devices))


def gather_kernel(w, gains, out, gains_out, send, recv, local):
    s, c, t, across, along, diagonal = plane_peers()
    to_x, to_y, to_d, to_core = (across, c, t), (along, c, t), (diagonal, c, t), (s, c, 1 - t)
    greet((to_x, to_y, to_d, to_core))
    rows = w.shape[1]
    upper = (rows // 2 + ROW_TILE - 1) // ROW_TILE * ROW_TILE
    parts = (pl.ds(0, upper), pl.ds(upper, rows - upper))

    def copy(src, dst, lane, k, device):
        return pltpu.make_async_remote_copy(
            src_ref=src,
            dst_ref=dst,
            send_sem=send.at[lane, k],
            recv_sem=recv.at[lane, k],
            device_id=device,
            device_id_type=MESH,
        )

    def own(lane, k):
        return copy(w.at[t, parts[k]], out.at[t, s, parts[k]], lane, k, (to_x, to_y)[lane])

    def onward(k):
        place = out.at[t, (across, along)[k], parts[k]]
        return copy(place, place, 2, k, (to_y, to_x)[k])

    def sideways(i, k):
        place = out.at[t, (across, along, diagonal)[i], parts[k]]
        return copy(place, place, 3 + i, k, to_core)

    def small(i):
        return copy(gains, gains_out.at[s], 6, i, (to_x, to_y, to_d)[i])

    keep = pltpu.make_async_copy(w, out.at[:, s], local.at[0])
    keep_gains = pltpu.make_async_copy(gains, gains_out.at[s], local.at[1])
    for k in range(2):
        own(0, k).start()
        own(1, 1 - k).start()
    for i in range(3):
        small(i).start()
    keep.start()
    keep_gains.start()
    own(0, 0).wait_recv()
    onward(0).start()
    own(1, 1).wait_recv()
    onward(1).start()
    sideways(0, 0).start()
    sideways(1, 1).start()
    own(0, 1).wait_recv()
    sideways(0, 1).start()
    own(1, 0).wait_recv()
    sideways(1, 0).start()
    for k in range(2):
        onward(k).wait_recv()
        sideways(2, k).start()
    for i in range(3):
        for k in range(2):
            sideways(i, k).wait()
        small(i).wait()
    for k in range(2):
        own(0, k).wait_send()
        own(1, k).wait_send()
        onward(k).wait_send()
    keep.wait()
    keep_gains.wait()


def gather_weights(w, gains):
    blocks, rows, cols = w.shape
    return pl.pallas_call(
        gather_kernel,
        out_shape=(
            jax.ShapeDtypeStruct((blocks, 4, rows, cols), BF16),
            jax.ShapeDtypeStruct((4,) + gains.shape, BF16),
        ),
        in_specs=[pl.BlockSpec(memory_space=pl.ANY)] * 2,
        out_specs=[pl.BlockSpec(memory_space=pl.ANY)] * 2,
        scratch_shapes=[
            pltpu.SemaphoreType.DMA((7, 3)),
            pltpu.SemaphoreType.DMA((7, 3)),
            pltpu.SemaphoreType.DMA((2,)),
        ],
        compiler_params=pltpu.CompilerParams(collective_id=0, has_side_effects=True),
        name="gather_weights",
    )(w, gains)


GROUP = QUERY_HEADS // KEY_VALUE_HEADS
SCORE_SCALE = 1.0 / math.sqrt(HEAD_SIZE)


def heads_of(ref, group):
    first = group * GROUP
    return jnp.concatenate(
        [ref[:, (first + i) * HEAD_SIZE : (first + i + 1) * HEAD_SIZE] for i in range(GROUP)], axis=0
    )


def side_by_side(stacked):
    rows = stacked.shape[0] // GROUP
    return [stacked[i * rows : (i + 1) * rows] for i in range(GROUP)]


def visible_keys(index_ref, keys):
    rows = index_ref.shape[0]
    column = lax.broadcasted_iota(jnp.int32, (rows, keys), 1)
    seen = (column >= index_ref[:, 1:2]) & (column <= index_ref[:, 0:1])
    bias = jnp.where(seen, 0.0, NEGATIVE_HUGE)
    return jnp.concatenate([bias] * GROUP, axis=0)


def contract(left, right, dims):
    return lax.dot_general(left, right, (dims, ((), ())), preferred_element_type=jnp.float32)


def softmax_of(query, key, bias):
    scores = contract(query, key, ((1,), (1,))) * SCORE_SCALE + bias
    exponent = jnp.exp(scores - jnp.max(scores, axis=-1, keepdims=True))
    return exponent * (1.0 / jnp.sum(exponent, axis=-1, keepdims=True))


def columns_of(group):
    return slice(group * HEAD_SIZE, (group + 1) * HEAD_SIZE)


def attend_kernel(index_ref, query_ref, kv_ref, out_ref):
    bias = visible_keys(index_ref, kv_ref.shape[0])
    parts = []
    for group in range(KEY_VALUE_HEADS):
        key = kv_ref[:, columns_of(group)]
        value = kv_ref[:, columns_of(KEY_VALUE_HEADS + group)]
        probs = softmax_of(heads_of(query_ref, group), key, bias).astype(BF16)
        parts += side_by_side(contract(probs, value, ((1,), (0,))))
    out_ref[...] = jnp.concatenate(parts, axis=1)


def attend_back_kernel(index_ref, query_ref, kv_ref, grad_ref, out_ref, query_grad_ref, kv_grad_ref):
    bias = visible_keys(index_ref, kv_ref.shape[0])
    query_parts, key_parts, value_parts = [], [], []
    for group in range(KEY_VALUE_HEADS):
        key = kv_ref[:, columns_of(group)]
        value = kv_ref[:, columns_of(KEY_VALUE_HEADS + group)]
        query = heads_of(query_ref, group)
        grad = heads_of(grad_ref, group)
        delta = jnp.sum(grad.astype(jnp.float32) * heads_of(out_ref, group), axis=-1, keepdims=True)
        probs = softmax_of(query, key, bias)
        probs_grad = contract(grad, value, ((1,), (1,)))
        scores_grad = (probs * (probs_grad - delta)).astype(BF16)
        query_parts += side_by_side(contract(scores_grad, key, ((1,), (0,))) * SCORE_SCALE)
        key_parts.append(contract(scores_grad, query, ((0,), (0,))) * SCORE_SCALE)
        value_parts.append(contract(probs.astype(BF16), grad, ((0,), (0,))))
    query_grad_ref[...] = jnp.concatenate(query_parts, axis=1)
    kv_grad_ref[...] = jnp.concatenate(key_parts + value_parts, axis=1).astype(BF16)


def attention_call(kernel, name, passes, out_shape, *operands):
    rows, keys = operands[1].shape[0], operands[2].shape[0]
    whole = pl.BlockSpec(memory_space=pltpu.VMEM)
    return pl.pallas_call(
        kernel,
        out_shape=out_shape,
        in_specs=[whole] * len(operands),
        out_specs=[whole] * len(out_shape),
        compiler_params=pltpu.CompilerParams(vmem_limit_bytes=40 * 1024 * 1024),
        cost_estimate=pl.CostEstimate(
            flops=passes * 4 * 2 * QUERY_HEADS * rows * keys * HEAD_SIZE,
            bytes_accessed=8 * 1024 * 1024,
            transcendentals=QUERY_HEADS * rows * keys,
        ),
        name=name,
    )(*operands)


ACROSS = ((0, 1), (1, 0), (2, 3), (3, 2))
ALONG = ((0, 2), (2, 0), (1, 3), (3, 1))


def swap(block, pairs):
    return lax.ppermute(block, "shard", pairs)


def plane_neighbours(block):
    return block, swap(block, ACROSS), swap(block, ALONG)


def plane_diagonal(near, x_first):
    return swap(near[1], ALONG) if x_first else swap(near[2], ACROSS)


def plane_join(near, from_d):
    s, c, t, across, along, diagonal = plane_peers()
    block, from_x, from_y = near
    whole = jnp.zeros((4,) + block.shape, block.dtype)
    for owner, part in ((s, block), (across, from_x), (along, from_y), (diagonal, from_d)):
        whole = lax.dynamic_update_index_in_dim(whole, part, owner, 0)
    return whole


def plane_first(blocks, x_first):
    s, c, t, across, along, diagonal = plane_peers()
    near, far, straight = (across, along, ACROSS) if x_first else (along, across, ALONG)

    def part(owner):
        return lax.dynamic_index_in_dim(blocks, owner, 0, keepdims=False)

    first = swap(part(diagonal), straight)
    summed = (part(far).astype(jnp.float32) + first.astype(jnp.float32)).astype(BF16)
    return summed, part(near), part(s)


def plane_scatter(summed, direct, kept):
    total = kept.astype(jnp.float32) + direct.astype(jnp.float32) + summed.astype(jnp.float32)
    return total.astype(BF16)


def reduce_kernel(
    n, chunks, attn, ffn, attn_out, ffn_out, side, first, partial, direct, summed, line, middle, carry, send, recv
):
    s, c, t, across, along, diagonal = plane_peers()
    half = n // 2
    inner = jnp.where(c < half, c + 1, c - 1)
    outer = jnp.where(c < half, c - 1, c + 1)
    to_x, to_y, to_core = (across, c, t), (along, c, t), (s, c, 1 - t)
    at_end = (c == 0) | (c == n - 1)
    at_middle = (c == half - 1) | (c == half)
    barrier = pltpu.get_barrier_semaphore()
    for device in (to_x, to_y, to_core, (s, inner, t)):
        pl.semaphore_signal(barrier, inc=1, device_id=device, device_id_type=MESH)

    @pl.when(jnp.logical_not(at_end))
    def _():
        pl.semaphore_signal(barrier, inc=1, device_id=(s, outer, t), device_id_type=MESH)
        pl.semaphore_wait(barrier, 5)

    @pl.when(at_end)
    def _():
        pl.semaphore_wait(barrier, 4)

    def copy(src, dst, lane, i, device):
        return pltpu.make_async_remote_copy(
            src_ref=src,
            dst_ref=dst,
            send_sem=send.at[lane, i],
            recv_sem=recv.at[lane, i],
            device_id=device,
            device_id_type=MESH,
        )

    count = len(chunks)
    attn_chunks = [i for i in range(count) if chunks[i][0] == 0]
    base = attn_chunks[0]

    def rows_of(i, buffer):
        return buffer.at[i, pl.ds(0, chunks[i][2])]

    def plane_rows(i, buffer):
        return buffer.at[i - base, pl.ds(0, chunks[i][2])]

    def mine(i, owner):
        k, start, size = chunks[i]
        return side.at[owner, pl.ds(start, size)]

    def result(i):
        k, start, size = chunks[i]
        if k == 0:
            return attn_out.at[t, pl.ds(start, size)]
        return ffn_out.at[k - 1, pl.ds(start, size)]

    def addend(i):
        k, start, size = chunks[i]
        return rows_of(i, carry) if k == 0 else ffn.at[k - 1, pl.ds(start, size)]

    def x_first(i):
        return (i - base) % 2 == 0

    def add(*refs):
        total = refs[0][...].astype(jnp.float32)
        for ref in refs[1:]:
            total = total + ref[...].astype(jnp.float32)
        return total.astype(BF16)

    def send_first(i):
        return copy(mine(i, diagonal), plane_rows(i, first), 0, i, to_x if x_first(i) else to_y)

    def send_direct(i):
        owner, device = (across, to_x) if x_first(i) else (along, to_y)
        return copy(mine(i, owner), plane_rows(i, direct), 1, i, device)

    def send_summed(i):
        return copy(plane_rows(i, partial), plane_rows(i, summed), 2, i, to_y if x_first(i) else to_x)

    def send_in(i):
        return copy(addend(i), rows_of(i, line), 3, i, (s, inner, t))

    def send_through(i):
        return copy(rows_of(i, carry), rows_of(i, line), 3, i, (s, inner, t))

    def send_middle(i):
        return copy(rows_of(i, carry), rows_of(i, middle), 4, i, (s, inner, t))

    def send_out(i):
        return copy(result(i), result(i), 5, i, (s, outer, t))

    def send_core(i):
        return copy(result(i), result(i), 6, i, to_core)

    def send_side():
        return copy(attn.at[1 - t], side, 7, 0, to_core)

    def start_in(i):
        @pl.when(at_end)
        def _():
            send_in(i).start()

    def stage_cores():
        send_side().wait()
        for owner in range(4):
            side[owner] = add(attn.at[t, owner], side.at[owner])
        for i in attn_chunks:
            send_first(i).start()
        for i in attn_chunks:
            send_direct(i).start()

    def stage_plane(i):
        send_first(i).wait_recv()
        owner = along if x_first(i) else across
        partial[i - base, pl.ds(0, chunks[i][2])] = add(mine(i, owner), plane_rows(i, first))
        send_summed(i).start()

    def stage_chips(i):
        send_direct(i).wait_recv()
        send_summed(i).wait_recv()
        carry[i, pl.ds(0, chunks[i][2])] = add(mine(i, s), plane_rows(i, direct), plane_rows(i, summed))
        start_in(i)

    def stage_fold(i):
        @pl.when(jnp.logical_not(at_end))
        def _():
            send_in(i).wait_recv()
            carry[i, pl.ds(0, chunks[i][2])] = add(addend(i), rows_of(i, line))

            @pl.when(at_middle)
            def _():
                send_middle(i).start()

            @pl.when(jnp.logical_not(at_middle))
            def _():
                send_through(i).start()

    def stage_total(i):
        @pl.when(at_middle)
        def _():
            send_middle(i).wait()
            result(i)[...] = add(rows_of(i, carry), rows_of(i, middle))

        @pl.when(jnp.logical_not(at_middle))
        def _():
            send_out(i).wait_recv()
            send_in(i).wait_send()

        @pl.when(jnp.logical_not(at_end))
        def _():
            send_out(i).start()

        if chunks[i][0] == 0:
            send_core(i).start()

    send_side().start()
    for i in range(base):
        start_in(i)
    for step in range(count + 1):
        if step == 2:
            stage_cores()
        if step == 4:
            for i in attn_chunks:
                stage_plane(i)
        if 6 <= step < 6 + len(attn_chunks):
            stage_chips(attn_chunks[step - 6])
        if step < count:
            stage_fold(step)
        if step >= 1:
            stage_total(step - 1)
    for i in range(count):
        if chunks[i][0] == 0:
            send_first(i).wait_send()
            send_direct(i).wait_send()
            send_summed(i).wait_send()
            send_core(i).wait()

        @pl.when(jnp.logical_not(at_end))
        def _():
            send_out(i).wait_send()


def reduce_grads(n, attn, ffn):
    attn_rows, ffn_rows, cols = attn.shape[2], ffn.shape[1], attn.shape[3]
    chunks = []
    for k in (1, 2, 3, 0):
        rows, pieces = (attn_rows, ATTN_CHUNKS) if k == 0 else (ffn_rows, FFN_CHUNKS)
        for j in range(pieces):
            chunks.append((k, j * (rows // pieces), rows // pieces))
    count, most = len(chunks), max(size for k, start, size in chunks)
    held = pltpu.VMEM((count, most, cols), BF16)
    plane_held = pltpu.VMEM((ATTN_CHUNKS, most, cols), BF16)
    return pl.pallas_call(
        functools.partial(reduce_kernel, n, tuple(chunks)),
        out_shape=(
            jax.ShapeDtypeStruct((2, attn_rows, cols), BF16),
            jax.ShapeDtypeStruct((3, ffn_rows, cols), BF16),
        ),
        in_specs=[pl.BlockSpec(memory_space=pltpu.VMEM)] * 2,
        out_specs=[pl.BlockSpec(memory_space=pltpu.VMEM)] * 2,
        scratch_shapes=[pltpu.VMEM((4, attn_rows, cols), BF16)]
        + [plane_held] * 4
        + [held] * 3
        + [pltpu.SemaphoreType.DMA((8, count)), pltpu.SemaphoreType.DMA((8, count))],
        compiler_params=pltpu.CompilerParams(
            collective_id=1, has_side_effects=True, vmem_limit_bytes=48 * 1024 * 1024
        ),
        name="reduce_grads",
    )(attn, ffn)


def rope_angles(position):
    halfway = HEAD_SIZE // 2
    frequency = jnp.exp(
        jnp.arange(halfway, dtype=jnp.float32) * (-2.0 * math.log(ROPE_BASE) / HEAD_SIZE)
    )
    angles = position.astype(jnp.float32)[:, None] * frequency[None, :]
    return (jnp.cos(angles)[:, None, :], jnp.sin(angles)[:, None, :])


def apply_rotary(vectors, cosine_table, sine_table):
    halfway = HEAD_SIZE // 2
    leading = vectors[..., :halfway]
    trailing = vectors[..., halfway:]
    return jnp.concatenate(
        [
            leading * cosine_table - trailing * sine_table,
            trailing * cosine_table + leading * sine_table,
        ],
        axis=-1,
    )


def unrotate(gradient, cosine_table, sine_table):
    halfway = HEAD_SIZE // 2
    leading = gradient[..., :halfway]
    trailing = gradient[..., halfway:]
    return jnp.concatenate(
        [
            leading * cosine_table + trailing * sine_table,
            trailing * cosine_table - leading * sine_table,
        ],
        axis=-1,
    )


def doc_starts(length_row, row_index):
    doc_ends = jnp.cumsum(length_row)
    before = jnp.where(doc_ends[None, :] <= row_index[:, None], length_row[None, :], 0)
    return jnp.sum(before, axis=1)


def rms_norm(values, gain_row):
    inverse = lax.rsqrt(jnp.mean(values * values, axis=-1, keepdims=True) + NORM_EPS)
    return (values * inverse * gain_row, inverse)


def norm_back(values, inverse, gain_row, gradient):
    unit_values = values * inverse
    scaled = gradient * gain_row
    gain_grad = jnp.sum(gradient * unit_values, axis=0)
    values_grad = inverse * (
        scaled - unit_values * jnp.mean(scaled * unit_values, axis=-1, keepdims=True)
    )
    return (gain_grad, values_grad)


def adam_step(weight, moment_one, moment_two, gradient, learning, decay_rate):
    first_new = BETA_ONE * moment_one + (1.0 - BETA_ONE) * gradient
    second_new = BETA_TWO * moment_two + (1.0 - BETA_TWO) * gradient * gradient
    first_hat = first_new / (1.0 - BETA_ONE**STEP)
    second_hat = second_new / (1.0 - BETA_TWO**STEP)
    weight_new = weight - learning * (
        first_hat / (jnp.sqrt(second_hat) + ADAM_EPS) + decay_rate * weight
    )
    return (weight_new, first_new, second_new)


def shards(
    tokens,
    cotangent,
    lengths,
    qkv_weight,
    qkv_first,
    qkv_second,
    out_weight,
    out_first,
    out_second,
    gate_up_weight,
    gate_up_first,
    gate_up_second,
    down_weight,
    down_first,
    down_second,
    norm_gains,
    gains_first,
    gains_second,
):
    shard_rows = tokens.shape[0]
    pack_groups = QUERY_HEADS // KEY_VALUE_HEADS
    qkv_low = qkv_weight.astype(jnp.bfloat16)
    out_low = out_weight.astype(jnp.bfloat16)
    gate_up_low = gate_up_weight.astype(jnp.bfloat16)
    down_low = down_weight.astype(jnp.bfloat16)
    gains_low = norm_gains.astype(jnp.bfloat16)
    plane = lax.axis_size("shard") == 4 and lax.axis_size("context") % 2 == 0
    width, hidden_units = MODEL_WIDTH + KEY_COLUMNS, down_weight.shape[0]
    plane = plane and hidden_units == width
    if plane:
        weights = jnp.stack(
            [qkv_low[:, :width], jnp.concatenate([qkv_low[:, width:], out_low], axis=1)]
        )
        own_gains = jnp.pad(gains_low, ((0, GAIN_ROWS - 2), (0, 0)))
        gathered, gains_parts = gather_weights(weights, own_gains)
        gathered, gains_parts, gate_low, up_low, down_low_t = lax.optimization_barrier(
            (gathered, gains_parts, gate_up_low[:, 0], gate_up_low[:, 1], down_low.T)
        )
        gathered = gathered.reshape(2, MODEL_WIDTH, width)
        qkv_mat = jnp.concatenate([gathered[0], gathered[1, :, :KEY_COLUMNS]], axis=1)
        out_mat = gathered[1, :, KEY_COLUMNS:]
        middle_column = hidden_units // 2
        neighbours = [
            plane_neighbours(block)
            for block in (
                gate_low,
                up_low,
                down_low_t[:, :middle_column],
                down_low_t[:, middle_column:],
            )
        ]
        diagonals = [
            plane_diagonal(near, x_first)
            for near, x_first in zip(neighbours, (True, False, True, False))
        ]
        gains_all = gains_parts[:, :2].transpose(1, 0, 2).reshape(2, MODEL_WIDTH)
    else:
        qkv_mat = lax.all_gather(qkv_low, "shard", axis=0, tiled=True)
        out_mat = lax.all_gather(out_low, "shard", axis=0, tiled=True)
        gate_up_mat = lax.all_gather(gate_up_low, "shard", axis=0, tiled=True)
        gate_mat, up_mat = gate_up_mat[:, 0], gate_up_mat[:, 1]
        down_mat_t = lax.all_gather(down_low, "shard", axis=1, tiled=True).T
        gains_all = lax.all_gather(gains_low, "shard", axis=1, tiled=True)
    gains_full = gains_all.astype(jnp.float32)
    tensor_size = lax.axis_size("tensor")
    offset = (lax.axis_index("context") * tensor_size + lax.axis_index("tensor")) * shard_rows
    row_index = offset + jnp.arange(shard_rows, dtype=jnp.int32)
    row_start = doc_starts(lengths[0], row_index)
    cosine_table, sine_table = rope_angles(row_index - row_start)
    inputs = tokens.astype(jnp.float32)
    normed_one, inverse_one = rms_norm(inputs, gains_full[0])
    first_low = normed_one.astype(jnp.bfloat16)
    projected_output = jnp.dot(first_low, qkv_mat, preferred_element_type=jnp.float32)
    query_low = (
        apply_rotary(
            projected_output[:, :MODEL_WIDTH].reshape(shard_rows, QUERY_HEADS, HEAD_SIZE),
            cosine_table,
            sine_table,
        )
        .astype(jnp.bfloat16)
        .reshape(shard_rows, KEY_VALUE_HEADS, pack_groups, HEAD_SIZE)
    )
    keys_low = (
        apply_rotary(
            projected_output[:, MODEL_WIDTH : MODEL_WIDTH + KEY_COLUMNS].reshape(
                shard_rows, KEY_VALUE_HEADS, HEAD_SIZE
            ),
            cosine_table,
            sine_table,
        )
        .astype(jnp.bfloat16)
        .reshape(shard_rows, KEY_COLUMNS)
    )
    kv_local = jnp.concatenate(
        [keys_low, projected_output[:, MODEL_WIDTH + KEY_COLUMNS :].astype(jnp.bfloat16)], axis=1
    )
    key_value_whole = lax.all_gather(kv_local, ("context", "tensor"), axis=0, tiled=True)
    total_keys = key_value_whole.shape[0]
    row_span = jnp.stack([row_index, row_start], axis=1)
    query_flat = query_low.reshape(shard_rows, MODEL_WIDTH)
    (attended_heads,) = attention_call(
        attend_kernel,
        "attend",
        2,
        (jax.ShapeDtypeStruct((shard_rows, MODEL_WIDTH), jnp.float32),),
        row_span,
        query_flat,
        key_value_whole,
    )
    if plane:
        attended_heads, diagonals = lax.optimization_barrier((attended_heads, diagonals))
        gate_mat, up_mat, down_left, down_right = (
            plane_join(near, far) for near, far in zip(neighbours, diagonals)
        )
        gate_mat = gate_mat.reshape(MODEL_WIDTH, hidden_units)
        up_mat = up_mat.reshape(MODEL_WIDTH, hidden_units)
        down_mat_t = jnp.concatenate([down_left, down_right], axis=2).reshape(
            MODEL_WIDTH, hidden_units
        )
    attended_low = attended_heads.astype(jnp.bfloat16)
    branch = jnp.dot(attended_low, out_mat, preferred_element_type=jnp.float32)
    hidden_state = inputs + branch
    normed_two, inverse_two = rms_norm(hidden_state, gains_full[1])
    second_low = normed_two.astype(jnp.bfloat16)
    ffn_rows = lax.all_gather(second_low, "tensor", axis=0, tiled=True)
    gate_vals = jnp.dot(ffn_rows, gate_mat, preferred_element_type=jnp.float32)
    upward = jnp.dot(ffn_rows, up_mat, preferred_element_type=jnp.float32)
    gate_sigmoid = jax.nn.sigmoid(gate_vals)
    activated = gate_vals * gate_sigmoid
    hidden_low = (activated * upward).astype(jnp.bfloat16)
    partial_out = jnp.einsum("tf,df->td", hidden_low, down_mat_t, preferred_element_type=jnp.float32)
    ffn_out = lax.psum_scatter(
        partial_out.astype(jnp.bfloat16), "tensor", scatter_dimension=0, tiled=True
    ).astype(jnp.float32)
    block_out = (hidden_state + ffn_out).astype(jnp.bfloat16)
    grad_rows = lax.all_gather(cotangent, "tensor", axis=0, tiled=True)
    down_grad_t = jnp.einsum("td,tf->df", grad_rows, hidden_low, preferred_element_type=jnp.float32)
    hidden_grad = jnp.dot(grad_rows, down_mat_t, preferred_element_type=jnp.float32)
    gate_grad = hidden_grad * upward * gate_sigmoid * (1.0 + gate_vals * (1.0 - gate_sigmoid))
    upward_grad = hidden_grad * activated
    gate_grad_low = gate_grad.astype(jnp.bfloat16)
    upward_grad_low = upward_grad.astype(jnp.bfloat16)
    gate_grad = jnp.einsum("td,tf->df", ffn_rows, gate_grad_low, preferred_element_type=jnp.float32)
    upward_grad = jnp.einsum(
        "td,tf->df", ffn_rows, upward_grad_low, preferred_element_type=jnp.float32
    )
    if plane:
        rows = MODEL_WIDTH // 4
        gate_blocks, up_blocks, down_blocks = (
            part.astype(jnp.bfloat16).reshape(4, rows, hidden_units)
            for part in (gate_grad, upward_grad, down_grad_t)
        )
        down_left, down_right = down_blocks[:, :, :middle_column], down_blocks[:, :, middle_column:]
        scatter_parts = [
            plane_first(blocks, x_first)
            for blocks, x_first in (
                (gate_blocks, True),
                (up_blocks, False),
                (down_left, True),
                (down_right, False),
            )
        ]
    normed_part = jnp.einsum(
        "tf,df->td", gate_grad_low, gate_mat, preferred_element_type=jnp.float32
    ) + jnp.einsum("tf,df->td", upward_grad_low, up_mat, preferred_element_type=jnp.float32)
    normed_two_grad = lax.psum_scatter(
        normed_part.astype(jnp.bfloat16), "tensor", scatter_dimension=0, tiled=True
    ).astype(jnp.float32)
    gain_two_grad, state_norm_grad = norm_back(
        hidden_state, inverse_two, gains_full[1], normed_two_grad
    )
    state_grad = cotangent.astype(jnp.float32) + state_norm_grad
    branch_low = state_grad.astype(jnp.bfloat16)
    out_grad = jnp.einsum("tk,td->kd", attended_low, branch_low, preferred_element_type=jnp.float32)
    attended_gradient = jnp.einsum(
        "td,kd->tk", branch_low, out_mat, preferred_element_type=jnp.float32
    )
    attended_gradient_narrow = attended_gradient.astype(jnp.bfloat16)
    if plane:
        attended_gradient_narrow, scatter_parts = lax.optimization_barrier(
            (attended_gradient_narrow, scatter_parts)
        )
        turns = ((ACROSS, ALONG), (ALONG, ACROSS), (ACROSS, ALONG), (ALONG, ACROSS))
        directs = [swap(parts[1], straight) for parts, (straight, turn) in zip(scatter_parts, turns)]
    query_grad, kv_terms = attention_call(
        attend_back_kernel,
        "attend_back",
        5,
        (
            jax.ShapeDtypeStruct((shard_rows, MODEL_WIDTH), jnp.float32),
            jax.ShapeDtypeStruct((total_keys, 2 * KEY_COLUMNS), jnp.bfloat16),
        ),
        row_span,
        query_flat,
        key_value_whole,
        attended_gradient_narrow,
        attended_heads,
    )
    if plane:
        kv_terms, query_grad, directs = lax.optimization_barrier((kv_terms, query_grad, directs))
        scattered = [
            plane_scatter(swap(parts[0], turn), direct, parts[2])
            for parts, direct, (straight, turn) in zip(scatter_parts, directs, turns)
        ]
    key_value_gradient = lax.psum_scatter(
        kv_terms, ("context", "tensor"), scatter_dimension=0, tiled=True
    ).astype(jnp.float32)
    key_back = unrotate(
        key_value_gradient[:, :KEY_COLUMNS].reshape(shard_rows, KEY_VALUE_HEADS, HEAD_SIZE),
        cosine_table,
        sine_table,
    ).reshape(shard_rows, KEY_COLUMNS)
    query_back = unrotate(
        query_grad.reshape(shard_rows, QUERY_HEADS, HEAD_SIZE), cosine_table, sine_table
    ).reshape(shard_rows, MODEL_WIDTH)
    projected_low = jnp.concatenate(
        [query_back, key_back, key_value_gradient[:, KEY_COLUMNS:]], axis=1
    ).astype(jnp.bfloat16)
    qkv_grad = jnp.einsum("td,tk->dk", first_low, projected_low, preferred_element_type=jnp.float32)
    normed_one_grad = jnp.einsum(
        "tk,dk->td", projected_low, qkv_mat, preferred_element_type=jnp.float32
    )
    gain_one_grad, input_norm_grad = norm_back(inputs, inverse_one, gains_full[0], normed_one_grad)
    tokens_grad = state_grad + input_norm_grad
    gains_grad = jnp.stack([gain_one_grad, gain_two_grad])
    if plane:
        rows = MODEL_WIDTH // 4
        attn_grad = jnp.stack(
            [
                qkv_grad[:, :width].astype(jnp.bfloat16),
                jnp.concatenate([qkv_grad[:, width:], out_grad], axis=1).astype(jnp.bfloat16),
            ]
        ).reshape(2, 4, rows, width)
        gain_rows = jnp.pad(
            gains_grad.astype(jnp.bfloat16).reshape(2, 4, rows).transpose(1, 0, 2),
            ((0, 0), (0, GAIN_ROWS - 2), (0, width - rows)),
        )
        gain_rows = jnp.stack([gain_rows, jnp.zeros_like(gain_rows)])
        attn_grad = jnp.concatenate([attn_grad, gain_rows], axis=2)
        ffn_grad = jnp.stack(
            [scattered[0], scattered[1], jnp.concatenate([scattered[2], scattered[3]], axis=1)]
        )
        attn_red, ffn_red = reduce_grads(lax.axis_size("context"), attn_grad, ffn_grad)
        gains_red = attn_red[0, rows : rows + 2, :rows].astype(jnp.float32)
        qkv_red = jnp.concatenate(
            [attn_red[0, :rows], attn_red[1, :rows, :KEY_COLUMNS]], axis=1
        ).astype(jnp.float32)
        out_red = attn_red[1, :rows, KEY_COLUMNS:].astype(jnp.float32)
        gate_up_red = jnp.stack([ffn_red[0], ffn_red[1]], axis=1).astype(jnp.float32)
        down_red = ffn_red[2].T.astype(jnp.float32)
    else:
        gate_up_grad = jnp.stack([gate_grad, upward_grad], axis=1)
        down_grad = down_grad_t.T
        qkv_part, out_part, gate_up_part, down_part, gains_part = (
            lax.psum_scatter(
                qkv_grad.astype(jnp.bfloat16), "shard", scatter_dimension=0, tiled=True
            ).astype(jnp.float32),
            lax.psum_scatter(
                out_grad.astype(jnp.bfloat16), "shard", scatter_dimension=0, tiled=True
            ).astype(jnp.float32),
            lax.psum_scatter(
                gate_up_grad.astype(jnp.bfloat16), "shard", scatter_dimension=0, tiled=True
            ).astype(jnp.float32),
            lax.psum_scatter(
                down_grad.astype(jnp.bfloat16), "shard", scatter_dimension=1, tiled=True
            ).astype(jnp.float32),
            lax.psum_scatter(
                gains_grad.astype(jnp.bfloat16), "shard", scatter_dimension=1, tiled=True
            ).astype(jnp.float32),
        )
        qkv_red, out_red, gains_red = (
            lax.psum(qkv_part.astype(jnp.bfloat16), ("context", "tensor")).astype(jnp.float32),
            lax.psum(out_part.astype(jnp.bfloat16), ("context", "tensor")).astype(jnp.float32),
            lax.psum(gains_part.astype(jnp.bfloat16), ("context", "tensor")).astype(jnp.float32),
        )
        gate_up_red, down_red = (
            lax.psum(gate_up_part.astype(jnp.bfloat16), "context").astype(jnp.float32),
            lax.psum(down_part.astype(jnp.bfloat16), "context").astype(jnp.float32),
        )
    results = adam_step(qkv_weight, qkv_first, qkv_second, qkv_red, RATES[0], DECAYS[0])
    results = results + adam_step(out_weight, out_first, out_second, out_red, RATES[1], DECAYS[1])
    results = results + adam_step(
        gate_up_weight, gate_up_first, gate_up_second, gate_up_red, RATES[2], DECAYS[2]
    )
    results = results + adam_step(
        down_weight, down_first, down_second, down_red, RATES[3], DECAYS[3]
    )
    results = results + adam_step(
        norm_gains, gains_first, gains_second, gains_red, RATES[4], DECAYS[4]
    )
    return (block_out, tokens_grad) + results


def solution(mesh):
    placed = (
        P(("shard", "context", "tensor"), None),
        P(("shard", "context", "tensor"), None),
        P("shard", None),
        P("shard", None),
        P("shard", None),
        P("shard", None),
        P("shard", None),
        P("shard", None),
        P("shard", None),
        P("shard", None, "tensor"),
        P("shard", None, "tensor"),
        P("shard", None, "tensor"),
        P("tensor", "shard"),
        P("tensor", "shard"),
        P("tensor", "shard"),
        P(None, "shard"),
        P(None, "shard"),
        P(None, "shard"),
    )
    return jax.shard_map(
        shards,
        mesh=mesh,
        in_specs=placed,
        out_specs=(
            P(("shard", "context", "tensor"), None),
            P(("shard", "context", "tensor"), None),
            P("shard", None),
            P("shard", None),
            P("shard", None),
            P("shard", None),
            P("shard", None),
            P("shard", None),
            P("shard", None, "tensor"),
            P("shard", None, "tensor"),
            P("shard", None, "tensor"),
            P("tensor", "shard"),
            P("tensor", "shard"),
            P("tensor", "shard"),
            P(None, "shard"),
            P(None, "shard"),
            P(None, "shard"),
        ),
        check_vma=False,
    )
```
